256 devices in a mesh: dom: 64 (over x, y, z_hi), sub: 4 (over z_lo, core).
Axes of the slice: x: 4, y: 4, z: 8 (z_hi: 4, z_lo: 2; z = z_hi * 2 + z_lo), core: 2. Of those that a mesh axis runs over, the one named last changes fastest.
Arguments:
- features: bfloat16 [64, 4, 2048, 128], P('dom', 'sub'), may hold values from -6 to 6
- offsets: int32 [3, 64, 4, 2048], P(None, 'dom', 'sub'), may hold values from 0 to 255, as said below
- frac: float32 [3, 64, 4, 2048], P(None, 'dom', 'sub'), may hold values from 0 to 0.999
- neighbors: int32 [64, 4, 2048, 16], P('dom', 'sub'), may hold values from 0 to 6143, as said below
- counts: int32 [64, 4, 2048], P('dom', 'sub'), may hold values from 1 to 16, as said below
- w_src: bfloat16 [128, 128], replicated, may hold values from -0.5 to 0.5
- w_dst: bfloat16 [128, 128], replicated, may hold values from -0.5 to 0.5
- w_rad: float32 [8, 128], replicated, may hold values from -3 to 3
- w_mid: bfloat16 [128, 128], replicated, may hold values from -0.5 to 0.5
- w_out: bfloat16 [384, 128], replicated, may hold values from -0.5 to 0.5
- w_charge: float32 [128], replicated, may hold values from -0.5 to 0.5
Outputs:
- new_features: bfloat16 [64, 4, 2048, 128], P('dom', 'sub')
- potential: float32 [64, 4, 2048], P('dom', 'sub')
The draws below stay inside these ranges and needn't reach their ends.
Inputs may be any that keep to these rules, and one draw needn't show every extreme that they name: `offsets`: component 0 of an atom of block (b, c) lies in [b * 4, (b + 1) * 4), component 1 in [c * 64, (c + 1) * 64). `neighbors`: an entry below 2048 names another atom of the same block, never the atom itself; a larger entry 2048 + r * 512 + s names atom s of the r-th of the eight surrounding blocks, taken in row-major order of their displacement along dom and sub with wrap-around; slot 0 of the first atom of every block holds the largest value. Slots at positions counts and later are padding; the first atom of every block has 16 live slots.
All inputs are finite; a program needn't handle non-finite values.
Results may differ from the reference program's by a relative error of at most 0.0052.
Values may be sent and summed in bfloat16 or wider, within the bound.
A program may use at most 128 MiB of HBM per device.

```python
import math
import jax
import jax.numpy as jnp
from jax import lax

CH = 128
GRID = 256
NRAD = 8
K = 16
ATOMS = 2048
HROWS = 512
BX = 64
BY = 4
LX = 4
LY = 64


def draw_offsets(key, part):
    key = jax.random.fold_in(key, 11)
    key_x, key_y, key_z, key_step = jax.random.split(key, 4)
    half_shape = (BX, BY, ATOMS // 2)
    block_x = lax.broadcasted_iota(jnp.int32, half_shape, 0)
    block_y = lax.broadcasted_iota(jnp.int32, half_shape, 1)
    base_x = block_x * LX + jax.random.randint(key_x, half_shape, 0, LX)
    base_y = block_y * LY + jax.random.randint(key_y, half_shape, 0, LY)
    base_z = jax.random.randint(key_z, half_shape, 0, GRID)
    steps = jax.random.randint(key_step, (3,) + half_shape, -1, 2)
    mate_x = jnp.minimum(jnp.maximum(base_x + steps[0], block_x * LX), block_x * LX + LX - 1)
    mate_y = jnp.minimum(jnp.maximum(base_y + steps[1], block_y * LY), block_y * LY + LY - 1)
    mate_z = (base_z + steps[2] + GRID) % GRID
    cell_x = jnp.stack([base_x, mate_x], axis=-1).reshape(BX, BY, ATOMS)
    cell_y = jnp.stack([base_y, mate_y], axis=-1).reshape(BX, BY, ATOMS)
    cell_z = jnp.stack([base_z, mate_z], axis=-1).reshape(BX, BY, ATOMS)
    return jnp.stack([cell_x, cell_y, cell_z]).astype(jnp.int32)


def draw_neighbors(key, part):
    key = jax.random.fold_in(key, 12)
    key_pick, key_own, key_far = jax.random.split(key, 3)
    shape_all = (BX, BY, ATOMS, K)
    atom_ids = lax.broadcasted_iota(jnp.int32, shape_all, 2)
    pick_far = jax.random.randint(key_pick, shape_all, 0, 2)
    own_pick = (atom_ids + 1 + jax.random.randint(key_own, shape_all, 0, ATOMS - 1)) % ATOMS
    far_pick = ATOMS + jax.random.randint(key_far, shape_all, 0, 8 * HROWS)
    chosen = jnp.where(pick_far == 1, far_pick, own_pick)
    chosen = chosen.at[:, :, 0, 0].set(ATOMS + 8 * HROWS - 1)
    return chosen.astype(jnp.int32)


def draw_counts(key, part):
    key = jax.random.fold_in(key, 13)
    key_load, key_slots = jax.random.split(key)
    raw_load = jax.random.randint(key_load, (BX, BY, 1), 0, K)
    block_load = K - raw_load * raw_load // (2 * K)
    lowest = jnp.maximum(block_load - K // 4, 1)
    filled = jax.random.randint(key_slots, (BX, BY, ATOMS), lowest, block_load + 1)
    filled = filled.at[:, :, 0].set(K)
    return filled.astype(jnp.int32)


def block_scale(key, shape, cuts, smallest, high):
    gain = 1.0
    for dim, parts in cuts:
        steps = jax.random.uniform(jax.random.fold_in(jax.random.fold_in(key, 6), dim), (parts,), jnp.float32, smallest / len(cuts), high / len(cuts))
        gain = gain * jnp.repeat(jnp.exp(steps), shape[dim] // parts).reshape((-1,) + (1,) * (len(shape) - 1 - dim))
    return gain


def normal_values(stream_key, shape, spread, reach, shards=(), kind=jnp.bfloat16):
    factor_of = block_scale(stream_key, shape, shards, -0.22, 0.18) if shards else 1.0
    values = jax.random.normal(stream_key, shape, jnp.float32) * spread * factor_of
    return jnp.minimum(jnp.maximum(values, -reach), reach).astype(kind)


def setup_inputs(seed: int = 0) -> dict:
    keys = jax.random.split(jax.random.key(seed), 12)
    features = normal_values(keys[0], (BX, BY, ATOMS, CH), 1.0, 6.0, ((0, 64), (1, 4)))
    offsets = draw_offsets(jax.random.fold_in(keys[11], 71), 0)
    frac = jnp.clip(0.999 * jax.random.uniform(keys[2], (3, BX, BY, ATOMS), jnp.float32) ** block_scale(keys[2], (3, BX, BY, ATOMS), ((1, 64), (2, 4)), -0.2, 0.2), 0.0, 0.999)
    neighbors = draw_neighbors(jax.random.fold_in(keys[11], 71), 0)
    counts = draw_counts(jax.random.fold_in(keys[11], 71), 0)
    w_src = normal_values(keys[5], (CH, CH), CH ** -0.5, 0.5)
    w_dst = normal_values(keys[6], (CH, CH), CH ** -0.5, 0.5)
    w_rad = normal_values(keys[7], (NRAD, CH), (NRAD // 2) ** -0.5, 3.0, (), jnp.float32)
    w_mid = normal_values(keys[8], (CH, CH), CH ** -0.5, 0.5)
    w_out = normal_values(keys[9], (3 * CH, CH), CH ** -0.5, 0.5)
    w_charge = normal_values(keys[10], (CH,), CH ** -0.5, 0.5, (), jnp.float32)
    return dict(features=features, offsets=offsets, frac=frac, neighbors=neighbors, counts=counts, w_src=w_src, w_dst=w_dst, w_rad=w_rad, w_mid=w_mid, w_out=w_out, w_charge=w_charge)


beta_ewald = 1.0
pot_scale = 16.0
cut_radius = 64.0
highest = lax.Precision.HIGHEST

def spline_weight(argument):
    cube_value = argument * argument * argument
    piece_one = cube_value / 6.0
    second = (-3.0 * cube_value + 12.0 * argument * argument - 12.0 * argument + 4.0) / 6.0
    piece_three = (3.0 * cube_value - 24.0 * argument * argument + 60.0 * argument - 44.0) / 6.0
    remain = 4.0 - argument
    fourth = remain * remain * remain / 6.0
    result = jnp.where(argument < 1.0, piece_one, jnp.where(argument < 2.0, second, jnp.where(argument < 3.0, piece_three, fourth)))
    return jnp.where((argument >= 0.0) & (argument < 4.0), result, jnp.zeros_like(result))

def wrap_cells(delta_cells, length):
    return (delta_cells + length // 2) % length - length // 2

def harmonics(direction):
    axis_x, axis_y, axis_z = (direction[0], direction[1], direction[2])
    root_three = math.sqrt(3.0)
    root_five = math.sqrt(5.0)
    root_fifteen = math.sqrt(15.0)
    return jnp.stack([jnp.ones_like(axis_x), root_three * axis_x, root_three * axis_y, root_three * axis_z, root_fifteen * axis_x * axis_y, root_fifteen * axis_y * axis_z, 0.5 * root_five * (3.0 * axis_z * axis_z - 1.0), root_fifteen * axis_x * axis_z, 0.5 * root_fifteen * (axis_x * axis_x - axis_y * axis_y)])

def edge_update(own_rows, src_term, dst_term, displace, live_slot, w_rad, w_mid, w_out):
    distance = jnp.sqrt(lax.optimization_barrier(jnp.sum(displace * displace, axis=0)) + 1.0)
    direction = displace / distance
    envelope = jnp.where(live_slot, 1.0 / (1.0 + (distance / cut_radius) ** 2), 0.0)
    lengths = 2.0 ** jnp.arange(w_rad.shape[0], dtype=jnp.float32)
    radial = jnp.exp(-distance[..., None] / lengths)
    radial_term = jnp.einsum('akn,nc->akc', radial, w_rad, precision=highest)
    latent = jax.nn.silu(src_term[:, None, :] + dst_term + radial_term).astype(jnp.bfloat16)
    flat_latent = latent.reshape(-1, latent.shape[2])
    hidden = jax.nn.silu(jnp.dot(flat_latent, w_mid, preferred_element_type=jnp.float32)).reshape(latent.shape)
    message = hidden * envelope[..., None]
    angular = harmonics(direction)
    moments = jnp.einsum('akc,mak->amc', message, angular, precision=highest)
    invariant = jnp.concatenate([moments[:, 0] ** 2, lax.optimization_barrier(jnp.sum(moments[:, 1:4] ** 2, axis=1)), lax.optimization_barrier(jnp.sum(moments[:, 4:9] ** 2, axis=1))], axis=-1).astype(jnp.bfloat16)
    update = jnp.dot(invariant, w_out, preferred_element_type=jnp.float32)
    return (own_rows.astype(jnp.float32) + update).astype(jnp.bfloat16)

def influence_axis(indices):
    signed = ((indices + GRID // 2) % GRID - GRID // 2).astype(jnp.float32) / GRID
    factor = (2.0 + jnp.cos(2.0 * math.pi / GRID * indices.astype(jnp.float32))) / 3.0
    return (signed * signed, factor * factor)

def influence_block(index_x, index_y, index_z):
    square_x, factor_x = influence_axis(index_x)
    square_y, factor_y = influence_axis(index_y)
    square_z, factor_z = influence_axis(index_z)
    squared = square_x[:, None, None] + square_y[None, :, None] + square_z[None, None, :]
    damping = factor_x[:, None, None] * factor_y[None, :, None] * factor_z[None, None, :]
    positive = squared > 0.0
    safe_square = jnp.where(positive, squared, 1.0)
    weighted = pot_scale * jnp.exp(-(math.pi ** 2 / beta_ewald ** 2) * squared) / (safe_square * damping)
    return jnp.where(positive, weighted, 0.0)

def reference(features, offsets, frac, neighbors, counts, w_src, w_dst, w_rad, w_mid, w_out, w_charge):
    flat_rows = features.reshape(-1, CH)
    src_all = jnp.dot(flat_rows, w_src, preferred_element_type=jnp.float32).reshape(BX, BY, ATOMS, CH)
    dst_all = jnp.dot(flat_rows, w_dst, preferred_element_type=jnp.float32).reshape(BX, BY, ATOMS, CH)
    raw_charge = jnp.dot(flat_rows.astype(jnp.float32), w_charge, precision=highest).reshape(BX, BY, ATOMS // 2, 2)
    half_gap = 0.5 * (raw_charge[..., 0] - raw_charge[..., 1])
    charges = jnp.stack([half_gap, -half_gap], axis=-1).reshape(BX, BY, ATOMS)
    slot_ids = jnp.arange(K, dtype=jnp.int32)

    def block_update(block_id):
        block_x = block_id // BY
        block_y = block_id % BY
        partner = neighbors[block_x, block_y]
        is_own = partner < ATOMS
        remote = jnp.maximum(partner - ATOMS, 0)
        neighbour_dir = remote // HROWS
        place_id = neighbour_dir + (neighbour_dir >= 4).astype(jnp.int32)
        part_x = jnp.where(is_own, block_x, (block_x + place_id // 3 - 1) % BX)
        part_y = jnp.where(is_own, block_y, (block_y + place_id % 3 - 1) % BY)
        part_atom = jnp.where(is_own, partner, remote % HROWS)
        dst_part = dst_all[part_x, part_y, part_atom]
        own_off = offsets[:, block_x, block_y]
        own_frac = frac[:, block_x, block_y]
        part_off = offsets[:, part_x, part_y, part_atom]
        part_frac = frac[:, part_x, part_y, part_atom]
        cell_shift = wrap_cells(part_off - own_off[:, :, None], GRID).astype(jnp.float32)
        displace = cell_shift + (part_frac - own_frac[:, :, None])
        live_slot = slot_ids[None, :] < counts[block_x, block_y][:, None]
        return edge_update(features[block_x, block_y], src_all[block_x, block_y], dst_part, displace, live_slot, w_rad, w_mid, w_out)
    new_features = lax.map(block_update, jnp.arange(BX * BY, dtype=jnp.int32)).reshape(BX, BY, ATOMS, CH)
    off_all = offsets.reshape(3, -1)
    frac_all = frac.reshape(3, -1)
    charge_flat = charges.reshape(-1)
    weight_lists = []
    cell_lists = []
    for axis_id in range(3):
        weight_lists.append([spline_weight(frac_all[axis_id] - float(offset_step) + 2.0) for offset_step in (-1, 0, 1, 2)])
        cell_lists.append([(off_all[axis_id] + offset_step) % GRID for offset_step in (-1, 0, 1, 2)])
    grid_flat = jnp.zeros((GRID * GRID * GRID,), jnp.float32)
    for index_x in range(4):
        for index_y in range(4):
            for index_z in range(4):
                flat_index = (cell_lists[0][index_x] * GRID + cell_lists[1][index_y]) * GRID + cell_lists[2][index_z]
                grid_flat = grid_flat.at[flat_index].add(charge_flat * weight_lists[0][index_x] * weight_lists[1][index_y] * weight_lists[2][index_z])
    charge_grid = grid_flat.reshape(GRID, GRID, GRID)
    full_ids = jnp.arange(GRID, dtype=jnp.int32)
    influence = influence_block(full_ids, full_ids, full_ids)
    spectrum = jnp.fft.fftn(charge_grid)
    potential_grid = jnp.real(jnp.fft.ifftn(spectrum * influence)).astype(jnp.float32)
    potential_flat = potential_grid.reshape(-1)
    potential = jnp.zeros_like(charge_flat)
    for index_x in range(4):
        for index_y in range(4):
            for index_z in range(4):
                flat_index = (cell_lists[0][index_x] * GRID + cell_lists[1][index_y]) * GRID + cell_lists[2][index_z]
                potential = potential + potential_flat[flat_index] * (weight_lists[0][index_x] * weight_lists[1][index_y] * weight_lists[2][index_z])
    return (new_features, potential.reshape(BX, BY, ATOMS))
```

```python
import functools
import math

import jax
import jax.numpy as jnp
import ml_dtypes
import numpy as np
from jax import lax
from jax.experimental import pallas as pl
from jax.experimental.pallas import tpu as pltpu
from jax.sharding import PartitionSpec as P

GRID = 256
ext_x = 7
ext_y = 67
rows_y = 72
head_rows = 512
table_pad = 8
halo_places = [(0, 0), (0, 1), (0, 2), (1, 0), (1, 2), (2, 0), (2, 1), (2, 2)]


def split_table(table):
    high = table.astype(ml_dtypes.bfloat16)
    low = (table - high.astype(np.float64)).astype(ml_dtypes.bfloat16)
    return high, low


def real_basis():
    cells = np.arange(GRID)
    basis = np.zeros((GRID, GRID))
    for k in range(GRID):
        wave = k if k <= GRID // 2 else k - GRID // 2
        angle = 2.0 * np.pi / GRID * ((wave * cells) % GRID)
        scale = math.sqrt((1.0 if k in (0, GRID // 2) else 2.0) / GRID)
        basis[k] = scale * (np.cos(angle) if k <= GRID // 2 else np.sin(angle))
    return basis


def wave_tables():
    index = np.arange(GRID)
    wave = np.where(index <= GRID // 2, index, index - GRID // 2) / GRID
    factor = (2.0 + np.cos(2.0 * np.pi * wave)) / 3.0
    return (wave**2).astype(np.float32), (1.0 / factor**2).astype(np.float32)


basis = real_basis()
columns_y = np.zeros((GRID, 4 * rows_y))
for c in range(4):
    for y in range(ext_y):
        columns_y[:, c * rows_y + y] = basis[:, (64 * c - 1 + y) % GRID]
columns_x = np.concatenate([basis[:, (4 * np.arange(64) - 1 + x) % GRID] for x in range(ext_x)], axis=1)
forward_z = split_table(basis.T.copy())
inverse_z = split_table(basis)
forward_y = split_table(columns_y)
inverse_y = split_table(columns_y.T.copy())
forward_x = split_table(columns_x)
inverse_x = split_table(columns_x.T.copy())
wave_square, wave_factor = wave_tables()

VMEM = pl.BlockSpec(memory_space=pltpu.VMEM)
SMEM = pl.BlockSpec(memory_space=pltpu.SMEM)
ANY = pl.BlockSpec(memory_space=pl.ANY)


def kernel_call(body, out_shape, in_specs, scratch=(), name=None, flops=0, moved=0):
    return pl.pallas_call(
        body,
        in_specs=in_specs,
        out_specs=jax.tree.map(lambda _: VMEM, out_shape),
        out_shape=out_shape,
        scratch_shapes=list(scratch),
        compiler_params=pltpu.CompilerParams(vmem_limit_bytes=40 * 2**20),
        cost_estimate=pl.CostEstimate(flops=flops, bytes_accessed=moved, transcendentals=0),
        name=name,
    )


def halves(x):
    high = x.astype(jnp.bfloat16)
    return high, (x - high.astype(jnp.float32)).astype(jnp.bfloat16)


def dot_split(a, b, pattern=(((1,), (0,)), ((), ()))):
    dot = functools.partial(lax.dot_general, dimension_numbers=pattern, preferred_element_type=jnp.float32)
    return dot(a[0], b[0]) + (dot(a[0], b[1]) + dot(a[1], b[0]))


def spline_four(f):
    g = 1.0 - f
    f2 = f * f
    f3 = f2 * f
    return (
        g * g * g * (1.0 / 6.0),
        (3.0 * f3 - 6.0 * f2 + 4.0) * (1.0 / 6.0),
        (-3.0 * f3 + 3.0 * f2 + 3.0 * f + 1.0) * (1.0 / 6.0),
        f3 * (1.0 / 6.0),
    )


def placed_weights(count, cell, f, wraps=False):
    ids = lax.broadcasted_iota(jnp.int32, (count, cell.shape[1]), 0)
    step = ids - cell
    if wraps:
        step = (step + 1) & (GRID - 1)
    result = jnp.zeros(step.shape, jnp.float32)
    for k, weight in enumerate(spline_four(f)):
        result = jnp.where(step == k, weight, result)
    return result


def pair_tiles(first, second, half):
    lane = lax.broadcasted_iota(jnp.int32, first.shape, 1)
    if half == 0:
        return jnp.where(lane < 64, first, pltpu.roll(second, 64, 1))
    return jnp.where(lane < 64, pltpu.roll(first, 64, 1), second)


def spread_kernel(cell_ref, frac_ref, feat_ref, w_ref, thi_ref, tlo_ref, out_ref, grid_s, charge_s):
    f32, bf16 = jnp.float32, jnp.bfloat16
    w = jnp.broadcast_to(w_ref[...], (16, 128))
    top = w.astype(bf16).astype(f32)
    mid = (w - top).astype(bf16).astype(f32)
    sub = lax.broadcasted_iota(jnp.int32, (16, 128), 0)
    parts = jnp.where(sub == 0, top, jnp.where(sub == 1, mid, jnp.where(sub == 2, w - top - mid, 0.0))).astype(bf16)
    raw = lax.dot_general(parts, feat_ref[...], (((1,), (1,)), ((), ())), preferred_element_type=f32)
    raw = jnp.broadcast_to(raw[0:1] + raw[1:2] + raw[2:3], (8, raw.shape[1]))
    atoms = raw.shape[1]
    lane = lax.broadcasted_iota(jnp.int32, raw.shape, 1)
    mate = jnp.where(lane % 2 == 0, pltpu.roll(raw, atoms - 1, 1), pltpu.roll(raw, 1, 1))
    charge_s[...] = 0.5 * (raw - mate)
    grid_s[...] = jnp.zeros_like(grid_s)

    def tile(i, carry):
        cols = pl.ds(pl.multiple_of(i * 512, 512), 512)
        along_x = placed_weights(8, cell_ref[0:1, cols], frac_ref[0:1, cols]) * charge_s[0:1, cols]
        along_y = placed_weights(rows_y, cell_ref[1:2, cols], frac_ref[1:2, cols])
        along_z = placed_weights(GRID, cell_ref[2:3, cols], frac_ref[2:3, cols], True)
        plane = jnp.concatenate([along_x[x : x + 1] * along_y for x in range(ext_x)], axis=0)
        grid_s[...] += dot_split(halves(plane), halves(along_z), (((1,), (1,)), ((), ())))
        return carry

    lax.fori_loop(0, atoms // 512, tile, 0)
    waves = dot_split(halves(grid_s[...]), (thi_ref[...], tlo_ref[...]))
    for q in range(4):
        for c in range(4):
            cols = slice(128 * (c // 2), 128 * (c // 2) + 128)
            first = waves[2 * q * rows_y : (2 * q + 1) * rows_y, cols]
            if 2 * q + 1 < ext_x:
                second = waves[(2 * q + 1) * rows_y : (2 * q + 2) * rows_y, cols]
            else:
                second = jnp.zeros_like(first)
            out_ref[c, :, q * 128 : q * 128 + 128] = pair_tiles(first, second, c % 2)


def forward_y_kernel(x_ref, thi_ref, tlo_ref, after_ref, out_ref):
    data = jnp.concatenate([x_ref[c] for c in range(4)], axis=0)
    waves = dot_split((thi_ref[...], tlo_ref[...]), halves(data))
    for j in range(4):
        out_ref[:, 0, j * 512 : j * 512 + 512] = waves[64 * j : 64 * j + 64]


def filter_kernel(x_ref, thi_ref, tlo_ref, uhi_ref, ulo_ref, col_ref, row_ref, after_ref, out_ref):
    slabs = [x_ref[:, 0, j * 512 : j * 512 + 512] for j in range(4)]
    pieces = []
    for x in range(ext_x):
        cols = slice(128 * (x // 2), 128 * (x // 2) + 128)
        pieces.append(
            jnp.concatenate(
                [pair_tiles(slabs[2 * p][:, cols], slabs[2 * p + 1][:, cols], x % 2) for p in range(2)], axis=1
            )
        )
    waves = dot_split((thi_ref[...], tlo_ref[...]), halves(jnp.concatenate(pieces, axis=0)))
    square = col_ref[0] + row_ref[0:1, :]
    factor = col_ref[1] * row_ref[1:2, :]
    positive = square > 0.0
    safe = jnp.where(positive, square, 1.0)
    influence = jnp.where(positive, 16.0 * jnp.exp(square * (-(math.pi**2))) / safe * factor, 0.0)
    cells = dot_split((uhi_ref[...], ulo_ref[...]), halves(waves * influence))
    for j in range(4):
        for q in range(4):
            cols = slice(128 * (j // 2), 128 * (j // 2) + 128)
            first = cells[128 * q : 128 * q + 64, cols]
            if 2 * q + 1 < ext_x:
                second = cells[128 * q + 64 : 128 * q + 128, cols]
            else:
                second = jnp.zeros_like(first)
            out_ref[:, 0, j * 512 + q * 128 : j * 512 + q * 128 + 128] = pair_tiles(first, second, j % 2)


def inverse_y_kernel(x_ref, thi_ref, tlo_ref, after_ref, out_ref):
    data = jnp.concatenate([x_ref[:, 0, j * 512 : j * 512 + 512] for j in range(4)], axis=0)
    cells = dot_split((thi_ref[...], tlo_ref[...]), halves(data))
    for c in range(4):
        out_ref[c] = cells[c * rows_y : (c + 1) * rows_y]


def read_kernel(x_ref, cell_ref, frac_ref, thi_ref, tlo_ref, after_ref, out_ref, grid_s):
    pieces = []
    for x in range(ext_x):
        cols = slice(128 * (x // 2), 128 * (x // 2) + 128)
        pieces.append(
            jnp.concatenate(
                [pair_tiles(x_ref[2 * p, :, cols], x_ref[2 * p + 1, :, cols], x % 2) for p in range(2)], axis=1
            )
        )
    grid_s[...] = dot_split(halves(jnp.concatenate(pieces, axis=0)), (thi_ref[...], tlo_ref[...]))

    def tile(i, carry):
        cols = pl.ds(pl.multiple_of(i * 512, 512), 512)
        along_x = placed_weights(8, cell_ref[0:1, cols], frac_ref[0:1, cols])
        along_y = placed_weights(rows_y, cell_ref[1:2, cols], frac_ref[1:2, cols])
        along_z = placed_weights(GRID, cell_ref[2:3, cols], frac_ref[2:3, cols], True)
        lines = dot_split(halves(grid_s[...]), halves(along_z))
        total = jnp.zeros(along_y.shape, jnp.float32)
        for x in range(ext_x):
            total = total + along_x[x : x + 1] * lines[x * rows_y : (x + 1) * rows_y]
        out_ref[:, cols] = jnp.sum(total * along_y, axis=0, keepdims=True)
        return carry

    lax.fori_loop(0, out_ref.shape[1] // 512, tile, 0)


def tables_kernel(own_ref, mid_ref, left_ref, right_ref, cell_ref, wsrc_ref, wdst_ref, tab_ref, src_ref, geo_ref):
    f32 = jnp.float32
    half = lambda ref: (ref[...].astype(f32) * 0.5).astype(jnp.bfloat16)
    w_src, w_dst = half(wsrc_ref), half(wdst_ref)
    own = own_ref[...]
    src_ref[...] = jnp.dot(own, w_src, preferred_element_type=f32)
    tab_ref[table_pad : table_pad + 2048, :] = jnp.dot(own, w_dst, preferred_element_type=f32)
    tab_ref[0:table_pad, :] = jnp.zeros((table_pad, 128), f32)
    tab_ref[table_pad + 6144 :, :] = jnp.zeros((table_pad, 128), f32)
    for c in range(3):
        geo_ref[c * 48 : c * 48 + 16, :] = cell_ref[c * 16 : c * 16 + 16, :]
    for r, (place_x, place_y) in enumerate(halo_places):
        ref = {0: left_ref, 1: mid_ref, 2: right_ref}[place_y]
        row = place_x if place_y != 1 else place_x // 2
        base = table_pad + 2048 + r * head_rows
        tab_ref[base : base + head_rows, :] = jnp.dot(ref[row, 0:head_rows, :], w_dst, preferred_element_type=f32)
        tail = ref[row, head_rows : head_rows + 48, :].astype(f32)
        for c in range(3):
            value = sum(tail[s * 12 + c * 4 : s * 12 + c * 4 + 4] for s in range(3))
            shift = (4.0 * (place_x - 1), 64.0 * (place_y - 1), 0.0)[c]
            geo_ref[c * 48 + 16 + r * 4 : c * 48 + 16 + r * 4 + 4, :] = value + shift


def edge_kernel(idx_ref, nb_ref, geo_ref, cnt_ref, tab_ref, src_ref, own_ref, wrad_ref, wmid_ref, wout_ref, after_ref, out_ref, ang_s, rad_s, inv_s, *, start, blocks):
    f32, bf16 = jnp.float32, jnp.bfloat16
    sub = lax.broadcasted_iota(jnp.int32, (8, 128), 0)
    lane = lax.broadcasted_iota(jnp.int32, (8, 128), 1)
    wr = wrad_ref[...] * 0.5
    wr_hi = wr.astype(bf16).astype(f32)
    w_ext = jnp.concatenate([wr_hi, wr_hi, wr - wr_hi, jnp.zeros_like(wr)], axis=0).astype(bf16)
    w_mid = (wmid_ref[...].astype(f32) * 0.5).astype(bf16)
    diag = (lane // 16) == sub

    def body(i, carry):
        g = start + i
        rows = pl.ds(pl.multiple_of(g * 8, 8), 8)
        nb = nb_ref[rows, :]
        low = nb & 127
        high = nb >> 7
        part = [jnp.zeros((8, 128), f32) for _ in range(3)]
        for h in range(48):
            hit = high == h
            for c in range(3):
                row = jnp.broadcast_to(geo_ref[c * 48 + h : c * 48 + h + 1, :], (8, 128))
                part[c] = jnp.where(hit, jnp.take_along_axis(row, low, axis=1), part[c])
        centre_lane = (g % 2) * 64 + sub * 8 + lane // 16
        mine = [
            jnp.take_along_axis(
                jnp.broadcast_to(geo_ref[pl.ds(c * 48 + g // 2, 1), :], (8, 128)), centre_lane, axis=1
            )
            for c in range(3)
        ]
        live = jnp.take_along_axis(
            jnp.broadcast_to(cnt_ref[pl.ds(g // 2, 1), :], (8, 128)), centre_lane, axis=1
        )
        dx = part[0] - mine[0]
        dy = part[1] - mine[1]
        dz = part[2] - mine[2]
        cells = jnp.floor(part[2]) - jnp.floor(mine[2])
        dz = jnp.where(cells >= 128.0, dz - 256.0, jnp.where(cells < -128.0, dz + 256.0, dz))
        squared = dx * dx + dy * dy + dz * dz + 1.0
        distance = jnp.sqrt(squared)
        inverse = 1.0 / distance
        nx, ny, nz = dx * inverse, dy * inverse, dz * inverse
        env = jnp.where((lane % 16) < live, 1.0 / (1.0 + squared * (1.0 / 4096.0)), 0.0)
        r3, r5, r15 = math.sqrt(3.0), math.sqrt(5.0), math.sqrt(15.0)
        ex, ey, ez = env * nx, env * ny, env * nz
        angular = [
            env, r3 * ex, r3 * ey, r3 * ez, r15 * ex * ny, r15 * ey * nz,
            (0.5 * r5) * (3.0 * ez * nz - env), r15 * ex * nz, (0.5 * r15) * (ex * nx - ey * ny),
        ]
        for m in range(9):
            ang_s[m] = angular[m]
        for j in range(8):
            rad_s[:, j, :] = jnp.exp(distance * (-1.0 / 2.0**j))
        gathered = []
        for t in range(128):
            acc = None
            for j in range(8):
                v = tab_ref[pl.ds(idx_ref[g * 1024 + (t * 8 + j)] + (table_pad - j), 8), :]
                acc = v if acc is None else jnp.where(sub == j, v, acc)
            gathered.append(acc)
        dst = jnp.concatenate(gathered, axis=0)
        pieces = []
        for r in range(8):
            rad = rad_s[r]
            rad_hi = rad.astype(bf16).astype(f32)
            pieces.append(jnp.concatenate([rad_hi, rad - rad_hi, rad_hi, jnp.zeros_like(rad)], axis=0).astype(bf16))
        rad_ext = jnp.concatenate(pieces, axis=1)
        term = lax.dot_general(rad_ext, w_ext, (((0,), (0,)), ((), ())), preferred_element_type=f32)
        src = src_ref[pl.ds(pl.multiple_of(g * 64, 64), 64), :]
        src = jnp.broadcast_to(src[:, None, :], (64, 16, 128)).reshape(1024, 128)
        half = dst + src + term
        latent = (half + half * jnp.tanh(half)).astype(bf16)
        half = jnp.dot(latent, w_mid, preferred_element_type=f32)
        hidden = half + half * jnp.tanh(half)
        hid_hi = hidden.astype(bf16)
        hid_lo = (hidden - hid_hi.astype(f32)).astype(bf16)
        hid = jnp.concatenate([hid_hi, hid_lo], axis=1)
        zero = jnp.zeros((8, 128), f32)
        for p in range(4):
            blocks_hi, blocks_lo = [], []
            for m in range(9):
                cols_hi, cols_lo = [], []
                for q in range(2):
                    row = jnp.where(diag, jnp.broadcast_to(ang_s[m, 2 * p + q : 2 * p + q + 1, :], (8, 128)), 0.0)
                    row_hi = row.astype(bf16).astype(f32)
                    row_lo = row - row_hi
                    cols_hi.append(jnp.concatenate([row_hi, zero] if q == 0 else [zero, row_hi], axis=0).astype(bf16))
                    cols_lo.append(jnp.concatenate([row_lo, zero] if q == 0 else [zero, row_lo], axis=0).astype(bf16))
                blocks_hi.append(jnp.concatenate(cols_hi, axis=1))
                blocks_lo.append(jnp.concatenate(cols_lo, axis=1))
            both = jnp.concatenate(blocks_hi + blocks_lo, axis=0)
            mom2 = jnp.dot(both, hid[p * 256 : p * 256 + 256], preferred_element_type=f32)
            mom = mom2[:144, :128] + mom2[:144, 128:] + mom2[144:, :128]
            sq = [mom[m * 16 : m * 16 + 16] ** 2 for m in range(9)]
            rr = slice(p * 16, p * 16 + 16)
            inv_s[rr, 0:128] = sq[0]
            inv_s[rr, 128:256] = sq[1] + sq[2] + sq[3]
            inv_s[rr, 256:384] = (sq[4] + sq[5]) + (sq[6] + sq[7]) + sq[8]
        update = jnp.dot(inv_s[...].astype(bf16), wout_ref[...], preferred_element_type=f32)
        arows = pl.ds(pl.multiple_of(g * 64, 64), 64)
        orows = pl.ds(pl.multiple_of(i * 64, 64), 64)
        out_ref[orows, :] = (own_ref[arows, :].astype(f32) + update).astype(bf16)
        return carry

    lax.fori_loop(0, blocks, body, 0)


def edge_call(start, blocks, idx, nb, geo, cnt, tab, src, own, w_rad, w_mid, w_out, after):
    return kernel_call(
        functools.partial(edge_kernel, start=start, blocks=blocks),
        jax.ShapeDtypeStruct((blocks * 64, 128), jnp.bfloat16),
        [SMEM] + [VMEM] * 9 + [ANY],
        [
            pltpu.VMEM((9, 8, 128), jnp.float32),
            pltpu.VMEM((8, 8, 128), jnp.float32),
            pltpu.VMEM((64, 384), jnp.float32),
        ],
        "edges",
        flops=blocks * 2 * 10**9,
        moved=blocks * 6 * 10**6,
    )(idx, nb, geo, cnt, tab, src, own, w_rad, w_mid, w_out, after)


def swap(x, axis):
    return lax.all_to_all(x, axis, split_axis=0, concat_axis=0, tiled=True)


def shifted(x, axis, step):
    size = lax.axis_size(axis)
    return lax.ppermute(x, axis, [(i, (i + step) % size) for i in range(size)])


def local(features, offsets, frac, neighbors, counts, w_src, w_dst, w_rad, w_mid, w_out, w_charge):
    f32, bf16 = jnp.float32, jnp.bfloat16
    own = features[0, 0]
    dom, sub = lax.axis_index("dom"), lax.axis_index("sub")
    anchor = jnp.stack([dom * 4, sub * 64, jnp.zeros_like(dom)]).astype(jnp.int32)
    cells = offsets[:, 0, 0] - anchor[:, None]
    fracs = frac[:, 0, 0]
    place = cells.astype(f32) + fracs
    place_rows = place.reshape(48, 128)

    head = place[:, :head_rows].reshape(12, 128)
    top = lax.reduce_precision(head, 8, 7)
    mid = lax.reduce_precision(head - top, 8, 7)
    low = lax.reduce_precision(head - top - mid, 8, 7)
    sent = jnp.concatenate(
        [own[:head_rows]] + [part.astype(bf16) for part in (top, mid, low)] + [jnp.zeros((12, 128), bf16)], axis=0
    )
    before = shifted(sent, "dom", 1)
    after = shifted(sent, "dom", -1)
    column = jnp.stack([before, sent, after])
    left = shifted(column, "sub", 1)
    right = shifted(column, "sub", -1)

    square, factor = jnp.asarray(wave_square), jnp.asarray(wave_factor)
    pick = lambda table: (table.reshape(4, 64)[:, dom][:, None], table.reshape(4, 64)[sub][None, :])
    square_y, square_z = pick(square)
    factor_y, factor_z = pick(factor)
    row = jnp.stack([(square_y + square_z).reshape(GRID), (factor_y * factor_z).reshape(GRID)])
    col = jnp.stack([square, factor])[:, :, None]

    grid_shape = jax.ShapeDtypeStruct((4, rows_y, 512), f32)
    pencil_shape = jax.ShapeDtypeStruct((64, 1, 2048), f32)
    ext_grid = pltpu.VMEM((ext_x * rows_y, GRID), f32)
    stage = functools.partial(kernel_call, flops=10**9, moved=10**6)

    waves_z = stage(
        spread_kernel, grid_shape, [VMEM] * 6, [ext_grid, pltpu.VMEM((8, 2048), f32)], "spread"
    )(cells, fracs, own, w_charge[None, :], *forward_z)
    tab, src, geo = stage(
        tables_kernel,
        (
            jax.ShapeDtypeStruct((6144 + 2 * table_pad, 128), f32),
            jax.ShapeDtypeStruct((2048, 128), f32),
            jax.ShapeDtypeStruct((144, 128), f32),
        ),
        [VMEM] * 7,
        (),
        "tables",
    )(own, jnp.stack([before, after]), left, right, place_rows, w_src, w_dst)
    pairs = neighbors[0, 0]
    idx, nb = pairs.reshape(-1), pairs.reshape(256, 128)
    live = counts[0, 0].reshape(16, 128)
    edges = lambda start, blocks, later: edge_call(
        start, blocks, idx, nb, geo, live, tab, src, own, w_rad, w_mid, w_out, later
    )
    done_a = edges(0, 8, waves_z)
    waves_y = stage(forward_y_kernel, pencil_shape, [VMEM] * 3 + [ANY], (), "forward_y")(
        swap(waves_z, "sub"), *forward_y, done_a
    )
    done_b = edges(8, 8, waves_y)
    filtered = stage(filter_kernel, pencil_shape, [VMEM] * 7 + [ANY], (), "filter")(
        swap(waves_y, "dom"), *forward_x, *inverse_x, col, row, done_b
    )
    done_c = edges(16, 8, filtered)
    cells_y = stage(inverse_y_kernel, grid_shape, [VMEM] * 3 + [ANY], (), "inverse_y")(
        swap(filtered, "dom"), *inverse_y, done_c
    )
    done_d = edges(24, 8, cells_y)
    potential = stage(
        read_kernel, jax.ShapeDtypeStruct((1, 2048), f32), [VMEM] * 5 + [ANY], [ext_grid], "read"
    )(swap(cells_y, "sub"), cells, fracs, *inverse_z, done_d)
    new_rows = jnp.concatenate([done_a, done_b, done_c, done_d], axis=0)
    return new_rows.reshape(features.shape), potential.reshape(1, 1, 2048)


def solution(mesh):
    placed = (
        P("dom", "sub", None, None),
        P(None, "dom", "sub", None),
        P(None, "dom", "sub", None),
        P("dom", "sub", None, None),
        P("dom", "sub", None),
        P(),
        P(),
        P(),
        P(),
        P(),
        P(),
    )
    return jax.shard_map(
        local,
        mesh=mesh,
        in_specs=placed,
        out_specs=(P("dom", "sub", None, None), P("dom", "sub", None)),
        check_vma=False,
    )
```

```python
import functools
import math

import jax
import jax.numpy as jnp
import ml_dtypes
import numpy as np
from jax import lax
from jax.experimental import pallas as pl
from jax.experimental.pallas import tpu as pltpu
from jax.sharding import PartitionSpec as P

GRID = 256
ext_x = 7
ext_y = 67
rows_y = 72
head_rows = 512
table_pad = 8
edge_split = (10, 21)
halo_places = [(0, 0), (0, 1), (0, 2), (1, 0), (1, 2), (2, 0), (2, 1), (2, 2)]


def split_table(table):
    high = table.astype(ml_dtypes.bfloat16)
    low = (table - high.astype(np.float64)).astype(ml_dtypes.bfloat16)
    return high, low


def real_basis():
    cells = np.arange(GRID)
    basis = np.zeros((GRID, GRID))
    for k in range(GRID):
        wave = k if k <= GRID // 2 else k - GRID // 2
        angle = 2.0 * np.pi / GRID * ((wave * cells) % GRID)
        scale = math.sqrt((1.0 if k in (0, GRID // 2) else 2.0) / GRID)
        basis[k] = scale * (np.cos(angle) if k <= GRID // 2 else np.sin(angle))
    return basis


def wave_tables():
    index = np.arange(GRID)
    wave = np.where(index <= GRID // 2, index, index - GRID // 2) / GRID
    factor = (2.0 + np.cos(2.0 * np.pi * wave)) / 3.0
    return (wave**2).astype(np.float32), (1.0 / factor**2).astype(np.float32)


basis = real_basis()
columns_y = np.zeros((GRID, 4 * rows_y))
for c in range(4):
    for y in range(ext_y):
        columns_y[:, c * rows_y + y] = basis[:, (64 * c - 1 + y) % GRID]
columns_x = np.concatenate([basis[:, (4 * np.arange(64) - 1 + x) % GRID] for x in range(ext_x)], axis=1)
forward_z = split_table(basis.T.copy())
inverse_z = split_table(basis)
forward_y = split_table(columns_y)
inverse_y = split_table(columns_y.T.copy())
forward_x = split_table(columns_x)
inverse_x = split_table(columns_x.T.copy())
wave_square, wave_factor = wave_tables()

def halves(x):
    high = x.astype(jnp.bfloat16)
    return high, (x - high.astype(jnp.float32)).astype(jnp.bfloat16)


def dot_split(a, b, pattern=(((1,), (0,)), ((), ()))):
    dot = functools.partial(lax.dot_general, dimension_numbers=pattern, preferred_element_type=jnp.float32)
    return dot(a[0], b[0]) + (dot(a[0], b[1]) + dot(a[1], b[0]))


def spline_four(f):
    g = 1.0 - f
    f2 = f * f
    f3 = f2 * f
    return (
        g * g * g * (1.0 / 6.0),
        (3.0 * f3 - 6.0 * f2 + 4.0) * (1.0 / 6.0),
        (-3.0 * f3 + 3.0 * f2 + 3.0 * f + 1.0) * (1.0 / 6.0),
        f3 * (1.0 / 6.0),
    )


def placed_weights(count, cell, f, wraps=False):
    ids = lax.broadcasted_iota(jnp.int32, (count, cell.shape[1]), 0)
    step = ids - cell
    if wraps:
        step = (step + 1) & (GRID - 1)
    result = jnp.zeros(step.shape, jnp.float32)
    for k, weight in enumerate(spline_four(f)):
        result = jnp.where(step == k, weight, result)
    return result


def pair_tiles(first, second, half):
    lane = lax.broadcasted_iota(jnp.int32, first.shape, 1)
    if half == 0:
        return jnp.where(lane < 64, first, pltpu.roll(second, 64, 1))
    return jnp.where(lane < 64, pltpu.roll(first, 64, 1), second)


def charge_row(feat_ref, w_ref):
    f32, bf16 = jnp.float32, jnp.bfloat16
    w = jnp.broadcast_to(w_ref[...], (16, 128))
    top = w.astype(bf16).astype(f32)
    mid = (w - top).astype(bf16).astype(f32)
    sub = lax.broadcasted_iota(jnp.int32, (16, 128), 0)
    parts = jnp.where(sub == 0, top, jnp.where(sub == 1, mid, jnp.where(sub == 2, w - top - mid, 0.0))).astype(bf16)
    raw = lax.dot_general(parts, feat_ref[...], (((1,), (1,)), ((), ())), preferred_element_type=f32)
    raw = jnp.broadcast_to(raw[0:1] + raw[1:2] + raw[2:3], (8, raw.shape[1]))
    lane = lax.broadcasted_iota(jnp.int32, raw.shape, 1)
    mate = jnp.where(lane % 2 == 0, pltpu.roll(raw, raw.shape[1] - 1, 1), pltpu.roll(raw, 1, 1))
    return 0.5 * (raw - mate)


def spread(cell_ref, frac_ref, charge_s, along_s, grid_s, table, out_ref):
    grid_s[...] = jnp.zeros_like(grid_s)

    def tile(i, carry):
        cols = pl.ds(pl.multiple_of(i * 512, 512), 512)
        along_x = placed_weights(8, cell_ref[0:1, cols], frac_ref[0:1, cols]) * charge_s[0:1, cols]
        along_y = placed_weights(rows_y, cell_ref[1:2, cols], frac_ref[1:2, cols])
        along_z = halves(placed_weights(GRID, cell_ref[2:3, cols], frac_ref[2:3, cols], True))
        along_s[0, :, cols] = along_z[0]
        along_s[1, :, cols] = along_z[1]
        plane = jnp.concatenate([along_x[x : x + 1] * along_y for x in range(ext_x)], axis=0)
        grid_s[...] += dot_split(halves(plane), along_z, (((1,), (1,)), ((), ())))
        return carry

    lax.fori_loop(0, 4, tile, 0)
    waves = dot_split(halves(grid_s[...]), table)
    for q in range(4):
        for c in range(4):
            cols = slice(128 * (c // 2), 128 * (c // 2) + 128)
            first = waves[2 * q * rows_y : (2 * q + 1) * rows_y, cols]
            if 2 * q + 1 < ext_x:
                second = waves[(2 * q + 1) * rows_y : (2 * q + 2) * rows_y, cols]
            else:
                second = jnp.zeros_like(first)
            out_ref[c, :, q * 128 : q * 128 + 128] = pair_tiles(first, second, c % 2)


def forward_y_step(x_ref, table, out_ref):
    waves = dot_split(table, halves(jnp.concatenate([x_ref[c] for c in range(4)], axis=0)))
    for j in range(4):
        out_ref[:, 0, j * 512 : j * 512 + 512] = waves[64 * j : 64 * j + 64]


def influence_block(col_ref, row_ref):
    square = col_ref[0] + row_ref[0:1, :]
    factor = col_ref[1] * row_ref[1:2, :]
    positive = square > 0.0
    safe = jnp.where(positive, square, 1.0)
    return jnp.where(positive, 16.0 * jnp.exp(square * (-(math.pi**2))) / safe * factor, 0.0)


def filter_step(x_ref, table, back, influence_ref, out_ref):
    slabs = [x_ref[:, 0, j * 512 : j * 512 + 512] for j in range(4)]
    pieces = []
    for x in range(ext_x):
        cols = slice(128 * (x // 2), 128 * (x // 2) + 128)
        pieces.append(
            jnp.concatenate(
                [pair_tiles(slabs[2 * p][:, cols], slabs[2 * p + 1][:, cols], x % 2) for p in range(2)], axis=1
            )
        )
    waves = dot_split(table, halves(jnp.concatenate(pieces, axis=0)))
    cells = dot_split(back, halves(waves * influence_ref[...]))
    for j in range(4):
        for q in range(4):
            cols = slice(128 * (j // 2), 128 * (j // 2) + 128)
            first = cells[128 * q : 128 * q + 64, cols]
            if 2 * q + 1 < ext_x:
                second = cells[128 * q + 64 : 128 * q + 128, cols]
            else:
                second = jnp.zeros_like(first)
            out_ref[:, 0, j * 512 + q * 128 : j * 512 + q * 128 + 128] = pair_tiles(first, second, j % 2)


def inverse_y_step(x_ref, table, out_ref):
    data = jnp.concatenate([x_ref[:, 0, j * 512 : j * 512 + 512] for j in range(4)], axis=0)
    cells = dot_split(table, halves(data))
    for c in range(4):
        out_ref[c] = cells[c * rows_y : (c + 1) * rows_y]


def read_step(x_ref, cell_ref, frac_ref, along_s, table, out_ref, grid_s):
    pieces = []
    for x in range(ext_x):
        cols = slice(128 * (x // 2), 128 * (x // 2) + 128)
        pieces.append(
            jnp.concatenate(
                [pair_tiles(x_ref[2 * p, :, cols], x_ref[2 * p + 1, :, cols], x % 2) for p in range(2)], axis=1
            )
        )
    grid_s[...] = dot_split(halves(jnp.concatenate(pieces, axis=0)), table)

    def tile(i, carry):
        cols = pl.ds(pl.multiple_of(i * 512, 512), 512)
        along_x = placed_weights(8, cell_ref[0:1, cols], frac_ref[0:1, cols])
        along_y = placed_weights(rows_y, cell_ref[1:2, cols], frac_ref[1:2, cols])
        lines = dot_split(halves(grid_s[...]), (along_s[0, :, cols], along_s[1, :, cols]))
        total = jnp.zeros(along_y.shape, jnp.float32)
        for x in range(ext_x):
            total = total + along_x[x : x + 1] * lines[x * rows_y : (x + 1) * rows_y]
        out_ref[:, cols] = jnp.sum(total * along_y, axis=0, keepdims=True)
        return carry

    lax.fori_loop(0, 4, tile, 0)


def geometry_step(g, nb_ref, cnt_ref, geo_s, ang_s, rad_s):
    f32 = jnp.float32
    sub = lax.broadcasted_iota(jnp.int32, (8, 128), 0)
    lane = lax.broadcasted_iota(jnp.int32, (8, 128), 1)
    rows = pl.ds(pl.multiple_of(g * 8, 8), 8)
    nb = nb_ref[rows, :]
    low = nb & 127
    high = nb >> 7
    part = [jnp.zeros((8, 128), f32) for _ in range(3)]
    for h in range(48):
        hit = high == h
        for c in range(3):
            row = jnp.broadcast_to(geo_s[c * 48 + h : c * 48 + h + 1, :], (8, 128))
            part[c] = jnp.where(hit, jnp.take_along_axis(row, low, axis=1), part[c])
    centre = (g % 2) * 64 + sub * 8 + lane // 16
    spot = lambda ref, row: jnp.take_along_axis(jnp.broadcast_to(ref[pl.ds(row, 1), :], (8, 128)), centre, axis=1)
    mine = [spot(geo_s, c * 48 + g // 2) for c in range(3)]
    live = spot(cnt_ref, g // 2)
    dx = part[0] - mine[0]
    dy = part[1] - mine[1]
    dz = part[2] - mine[2]
    cells = jnp.floor(part[2]) - jnp.floor(mine[2])
    dz = jnp.where(cells >= 128.0, dz - 256.0, jnp.where(cells < -128.0, dz + 256.0, dz))
    squared = dx * dx + dy * dy + dz * dz + 1.0
    distance = jnp.sqrt(squared)
    inverse = 1.0 / distance
    nx, ny, nz = dx * inverse, dy * inverse, dz * inverse
    env = jnp.where((lane % 16) < live, 1.0 / (1.0 + squared * (1.0 / 4096.0)), 0.0)
    r3, r5, r15 = math.sqrt(3.0), math.sqrt(5.0), math.sqrt(15.0)
    ex, ey, ez = env * nx, env * ny, env * nz
    angular = [
        env, r3 * ex, r3 * ey, r3 * ez, r15 * ex * ny, r15 * ey * nz,
        (0.5 * r5) * (3.0 * ez * nz - env), r15 * ex * nz, (0.5 * r15) * (ex * nx - ey * ny),
    ]
    for m in range(9):
        ang_s[m, rows, :] = angular[m]
    for j in range(8):
        rad_s[rows, j, :] = jnp.exp(distance * (-1.0 / 2.0**j))


def edge_step(g, w_ext, w_mid, w_out, idx_ref, own_ref, tab_s, src_s, ang_s, rad_s, inv_s, out_ref):
    f32, bf16 = jnp.float32, jnp.bfloat16
    sub = lax.broadcasted_iota(jnp.int32, (8, 128), 0)
    diag = (lax.broadcasted_iota(jnp.int32, (8, 128), 1) // 16) == sub
    gathered = []
    for t in range(128):
        acc = None
        for j in range(8):
            v = tab_s[pl.ds(idx_ref[g * 1024 + (t * 8 + j)] + (table_pad - j), 8), :]
            acc = v if acc is None else jnp.where(sub == j, v, acc)
        gathered.append(acc)
    dst = jnp.concatenate(gathered, axis=0)
    pieces = []
    for r in range(8):
        rad = rad_s[g * 8 + r]
        rad_hi = rad.astype(bf16).astype(f32)
        pieces.append(jnp.concatenate([rad_hi, rad - rad_hi, rad_hi, jnp.zeros_like(rad)], axis=0).astype(bf16))
    rad_ext = jnp.concatenate(pieces, axis=1)
    term = lax.dot_general(rad_ext, w_ext, (((0,), (0,)), ((), ())), preferred_element_type=f32)
    arows = pl.ds(pl.multiple_of(g * 64, 64), 64)
    src = jnp.broadcast_to(src_s[arows, :][:, None, :], (64, 16, 128)).reshape(1024, 128)
    half = dst + src + term
    latent = (half + half * jnp.tanh(half)).astype(bf16)
    half = jnp.dot(latent, w_mid, preferred_element_type=f32)
    hidden = half + half * jnp.tanh(half)
    hid = jnp.concatenate(halves(hidden), axis=1)
    zero = jnp.zeros((8, 128), f32)
    for p in range(4):
        blocks_hi, blocks_lo = [], []
        for m in range(9):
            cols_hi, cols_lo = [], []
            for q in range(2):
                line = ang_s[m, pl.ds(g * 8 + (2 * p + q), 1), :]
                row = jnp.where(diag, jnp.broadcast_to(line, (8, 128)), 0.0)
                row_hi = row.astype(bf16).astype(f32)
                row_lo = row - row_hi
                cols_hi.append(jnp.concatenate([row_hi, zero] if q == 0 else [zero, row_hi], axis=0).astype(bf16))
                cols_lo.append(jnp.concatenate([row_lo, zero] if q == 0 else [zero, row_lo], axis=0).astype(bf16))
            blocks_hi.append(jnp.concatenate(cols_hi, axis=1))
            blocks_lo.append(jnp.concatenate(cols_lo, axis=1))
        both = jnp.concatenate(blocks_hi + blocks_lo, axis=0)
        mom2 = jnp.dot(both, hid[p * 256 : p * 256 + 256], preferred_element_type=f32)
        mom = mom2[:144, :128] + mom2[:144, 128:] + mom2[144:, :128]
        sq = [mom[m * 16 : m * 16 + 16] ** 2 for m in range(9)]
        rows = slice(p * 16, p * 16 + 16)
        inv_s[rows, 0:128] = sq[0]
        inv_s[rows, 128:256] = sq[1] + sq[2] + sq[3]
        inv_s[rows, 256:384] = (sq[4] + sq[5]) + (sq[6] + sq[7]) + sq[8]
    update = jnp.dot(inv_s[...].astype(bf16), w_out, preferred_element_type=f32)
    out_ref[arows, :] = (own_ref[arows, :].astype(f32) + update).astype(bf16)


def layer_kernel(
    idx_ref, nb_ref, cnt_ref, own_ref, place_ref, head_ref, cell_ref, frac_ref, col_ref, row_ref,
    wsrc_ref, wdst_ref, wrad_ref, wmid_ref, wout_ref, wcharge_ref,
    fz0, fz1, fy0, fy1, fx0, fx1, ux0, ux1, uy0, uy1, uz0, uz1,
    new_ref, pot_ref,
    feat_halo, geo_halo, zsend, zrecv, ysend, yrecv, xsend, xrecv, isend, irecv,
    tab_s, src_s, geo_s, ang_s, rad_s, inv_s, grid_s, charge_s, along_s, influence_s,
    feat_send, feat_recv, geo_send, geo_recv, zs_sem, zr_sem, ys_sem, yr_sem, xs_sem, xr_sem, is_sem, ir_sem,
):
    f32, bf16 = jnp.float32, jnp.bfloat16
    me, part = lax.axis_index("dom"), lax.axis_index("sub")
    doms, subs = 64, 4
    turn = lambda x, step, size: lax.rem(x + (step + size), size)

    barrier = pltpu.get_barrier_semaphore()

    def greet(dom, sub):
        pl.semaphore_signal(barrier, inc=1, device_id=(dom, sub), device_id_type=pl.DeviceIdType.MESH)

    for step_x in (-1, 1):
        for step_y in (-1, 1):
            greet(turn(me, step_x, doms), turn(part, step_y, subs))
    for step in range(1, subs):
        greet(me, turn(part, step, subs))

    def greet_dom(step, carry):
        greet(lax.rem(me + step, doms), part)
        return carry

    lax.fori_loop(1, doms, greet_dom, 0)
    pl.semaphore_wait(barrier, 4 + subs - 1 + doms - 1)

    def remote(src, dst, send, recv, dom, sub):
        return pltpu.make_async_remote_copy(
            src_ref=src, dst_ref=dst, send_sem=send, recv_sem=recv,
            device_id=(dom, sub), device_id_type=pl.DeviceIdType.MESH,
        )

    geo_copies = []
    for r, (place_x, place_y) in enumerate(halo_places):
        target = (turn(me, 1 - place_x, doms), turn(part, 1 - place_y, subs))
        geo_copies.append(remote(head_ref, geo_halo.at[r], geo_send.at[r], geo_recv.at[r], *target))

    def feat_copy(src, place_x, place_y):
        r = halo_places.index((place_x, place_y))
        if (place_x, place_y) in ((0, 1), (2, 1)):
            target = (turn(me, 1 - place_x, doms), part)
        else:
            target = (me, turn(part, 1 - place_y, subs))
        return remote(src, feat_halo.at[r], feat_send.at[r], feat_recv.at[r], *target)

    rows = own_ref.at[pl.ds(0, head_rows)]
    first = [feat_copy(rows, 0, 1), feat_copy(rows, 2, 1), feat_copy(rows, 1, 0), feat_copy(rows, 1, 2)]
    slot = lambda x, y: feat_halo.at[halo_places.index((x, y))]
    second = [feat_copy(slot(x, 1), x, y) for x in (0, 2) for y in (0, 2)]
    for copy in geo_copies + first:
        copy.start()

    def swap_sub(src, dst, send, recv):
        return [
            remote(src.at[turn(part, step, subs)], dst.at[part], send.at[step - 1], recv.at[step - 1],
                   me, turn(part, step, subs))
            for step in range(1, subs)
        ]

    def dom_copy(src, dst, send, recv, step):
        target = lax.rem(me + step, doms)
        return remote(src.at[target], dst.at[me], send.at[step - 1], recv.at[step - 1], target, part)

    def swap_dom(src, dst, send, recv):
        def start(step, carry):
            dom_copy(src, dst, send, recv, step).start()
            return carry

        lax.fori_loop(1, doms, start, 0)
        dst[me] = src[me]

    def dom_wait(src, dst, send, recv, which):
        def wait(step, carry):
            getattr(dom_copy(src, dst, send, recv, step), which)()
            return carry

        lax.fori_loop(1, doms, wait, 0)

    charge_s[...] = charge_row(own_ref, wcharge_ref)
    spread(cell_ref, frac_ref, charge_s, along_s, grid_s, (fz0[...], fz1[...]), zsend)
    z_copies = swap_sub(zsend, zrecv, zs_sem, zr_sem)
    for copy in z_copies:
        copy.start()
    zrecv[part] = zsend[part]

    halved = lambda ref: (ref[...].astype(f32) * 0.5).astype(bf16)
    w_src, w_dst, w_mid, w_out = halved(wsrc_ref), halved(wdst_ref), halved(wmid_ref), wout_ref[...]
    wr = wrad_ref[...] * 0.5
    wr_hi = wr.astype(bf16).astype(f32)
    w_ext = jnp.concatenate([wr_hi, wr_hi, wr - wr_hi, jnp.zeros_like(wr)], axis=0).astype(bf16)
    src_s[...] = jnp.dot(own_ref[...], w_src, preferred_element_type=f32)
    tab_s[table_pad : table_pad + 2048, :] = jnp.dot(own_ref[...], w_dst, preferred_element_type=f32)
    tab_s[0:table_pad, :] = jnp.zeros((table_pad, 128), f32)
    tab_s[table_pad + 6144 :, :] = jnp.zeros((table_pad, 128), f32)
    influence_s[...] = influence_block(col_ref, row_ref)
    for copy in geo_copies:
        copy.wait_recv()
    for c in range(3):
        geo_s[c * 48 : c * 48 + 16, :] = place_ref[c * 16 : c * 16 + 16, :]
        for r, (place_x, place_y) in enumerate(halo_places):
            shift = (4.0 * (place_x - 1), 64.0 * (place_y - 1), 0.0)[c]
            at = c * 48 + 16 + r * 4
            geo_s[at : at + 4, :] = geo_halo[r, c * 4 : c * 4 + 4, :] + shift

    def geometry(g, carry):
        geometry_step(2 * g, nb_ref, cnt_ref, geo_s, ang_s, rad_s)
        geometry_step(2 * g + 1, nb_ref, cnt_ref, geo_s, ang_s, rad_s)
        return carry

    lax.fori_loop(0, 6, geometry, 0)
    for copy in first[:2]:
        copy.wait_recv()
    for copy in second:
        copy.start()
    lax.fori_loop(6, 16, geometry, 0)

    for copy in z_copies:
        copy.wait_recv()
    forward_y_step(zrecv, (fy0[...], fy1[...]), ysend)
    swap_dom(ysend, yrecv, ys_sem, yr_sem)

    for copy in first[2:] + second:
        copy.wait_recv()
    for r in range(8):
        base = table_pad + 2048 + r * head_rows
        tab_s[base : base + head_rows, :] = jnp.dot(feat_halo[r], w_dst, preferred_element_type=f32)

    i_copies = swap_sub(isend, irecv, is_sem, ir_sem)

    def edges(g, carry):
        @pl.when(g == edge_split[0])
        def _():
            dom_wait(ysend, yrecv, ys_sem, yr_sem, "wait_recv")
            filter_step(yrecv, (fx0[...], fx1[...]), (ux0[...], ux1[...]), influence_s, xsend)
            swap_dom(xsend, xrecv, xs_sem, xr_sem)

        @pl.when(g == edge_split[1])
        def _():
            dom_wait(xsend, xrecv, xs_sem, xr_sem, "wait_recv")
            inverse_y_step(xrecv, (uy0[...], uy1[...]), isend)
            for copy in i_copies:
                copy.start()
            irecv[part] = isend[part]

        edge_step(g, w_ext, w_mid, w_out, idx_ref, own_ref, tab_s, src_s, ang_s, rad_s, inv_s, new_ref)
        return carry

    lax.fori_loop(0, 32, edges, 0)
    for copy in i_copies:
        copy.wait_recv()
    read_step(irecv, cell_ref, frac_ref, along_s, (uz0[...], uz1[...]), pot_ref, grid_s)
    for copy in geo_copies + first + second + z_copies + i_copies:
        copy.wait_send()
    dom_wait(ysend, yrecv, ys_sem, yr_sem, "wait_send")
    dom_wait(xsend, xrecv, xs_sem, xr_sem, "wait_send")


def local(features, offsets, frac, neighbors, counts, w_src, w_dst, w_rad, w_mid, w_out, w_charge):
    f32, bf16 = jnp.float32, jnp.bfloat16
    own = features[0, 0]
    dom, sub = lax.axis_index("dom"), lax.axis_index("sub")
    anchor = jnp.stack([dom * 4, sub * 64, jnp.zeros_like(dom)]).astype(jnp.int32)
    cells = offsets[:, 0, 0] - anchor[:, None]
    fracs = frac[:, 0, 0]
    place = cells.astype(f32) + fracs
    head = jnp.concatenate([place[:, :head_rows].reshape(12, 128), jnp.zeros((4, 128), f32)], axis=0)

    square, factor = jnp.asarray(wave_square), jnp.asarray(wave_factor)
    pick = lambda table: (table.reshape(4, 64)[:, dom][:, None], table.reshape(4, 64)[sub][None, :])
    square_y, square_z = pick(square)
    factor_y, factor_z = pick(factor)
    row = jnp.stack([(square_y + square_z).reshape(GRID), (factor_y * factor_z).reshape(GRID)])
    col = jnp.stack([square, factor])[:, :, None]

    pairs = neighbors[0, 0]
    operands = (
        pairs.reshape(-1), pairs.reshape(256, 128), counts[0, 0].reshape(16, 128), own, place.reshape(48, 128), head,
        cells, fracs, col, row, w_src, w_dst, w_rad, w_mid, w_out, w_charge[None, :],
        *forward_z, *forward_y, *forward_x, *inverse_x, *inverse_y, *inverse_z,
    )
    vmem = pl.BlockSpec(memory_space=pltpu.VMEM)
    smem = pl.BlockSpec(memory_space=pltpu.SMEM)
    dma = pltpu.SemaphoreType.DMA
    slabs = pltpu.VMEM((4, rows_y, 512), f32)
    pencils = pltpu.VMEM((64, 1, 2048), f32)
    new_rows, potential = pl.pallas_call(
        layer_kernel,
        in_specs=[smem] + [vmem] * (len(operands) - 1),
        out_specs=(vmem, vmem),
        out_shape=(jax.ShapeDtypeStruct((2048, 128), bf16), jax.ShapeDtypeStruct((1, 2048), f32)),
        scratch_shapes=[
            pltpu.VMEM((8, head_rows, 128), bf16), pltpu.VMEM((8, 16, 128), f32),
            slabs, slabs, pencils, pencils, pencils, pencils, slabs, slabs,
            pltpu.VMEM((6144 + 2 * table_pad, 128), f32), pltpu.VMEM((2048, 128), f32), pltpu.VMEM((144, 128), f32),
            pltpu.VMEM((9, 256, 128), f32), pltpu.VMEM((256, 8, 128), f32), pltpu.VMEM((64, 384), f32),
            pltpu.VMEM((ext_x * rows_y, GRID), f32), pltpu.VMEM((8, 2048), f32), pltpu.VMEM((2, GRID, 2048), bf16),
            pltpu.VMEM((GRID, GRID), f32),
            dma((8,)), dma((8,)), dma((8,)), dma((8,)), dma((3,)), dma((3,)),
            dma((63,)), dma((63,)), dma((63,)), dma((63,)), dma((3,)), dma((3,)),
        ],
        compiler_params=pltpu.CompilerParams(
            vmem_limit_bytes=50 * 2**20, collective_id=0, has_side_effects=True
        ),
        name="layer",
    )(*operands)
    return new_rows.reshape(features.shape), potential.reshape(1, 1, 2048)


def solution(mesh):
    placed = (
        P("dom", "sub", None, None),
        P(None, "dom", "sub", None),
        P(None, "dom", "sub", None),
        P("dom", "sub", None, None),
        P("dom", "sub", None),
        P(),
        P(),
        P(),
        P(),
        P(),
        P(),
    )
    return jax.shard_map(
        local,
        mesh=mesh,
        in_specs=placed,
        out_specs=(P("dom", "sub", None, None), P("dom", "sub", None)),
        check_vma=False,
    )
```

```python
import functools
import math

import jax
import jax.numpy as jnp
import ml_dtypes
import numpy as np
from jax import lax
from jax.experimental import pallas as pl
from jax.experimental.pallas import tpu as pltpu
from jax.sharding import PartitionSpec as P

GRID = 256
ext_x = 7
ext_y = 67
rows_y = 72
rows_back = 80
head_rows = 512
table_pad = 8
edge_split = (6, 11)
halo_places = [(0, 0), (0, 1), (0, 2), (1, 0), (1, 2), (2, 0), (2, 1), (2, 2)]


def split_table(table):
    high = table.astype(ml_dtypes.bfloat16)
    low = (table - high.astype(np.float64)).astype(ml_dtypes.bfloat16)
    return high, low


def real_basis():
    cells = np.arange(GRID)
    basis = np.zeros((GRID, GRID))
    for k in range(GRID):
        wave = k if k <= GRID // 2 else k - GRID // 2
        angle = 2.0 * np.pi / GRID * ((wave * cells) % GRID)
        scale = math.sqrt((1.0 if k in (0, GRID // 2) else 2.0) / GRID)
        basis[k] = scale * (np.cos(angle) if k <= GRID // 2 else np.sin(angle))
    return basis


def wave_tables():
    index = np.arange(GRID)
    wave = np.where(index <= GRID // 2, index, index - GRID // 2) / GRID
    factor = (2.0 + np.cos(2.0 * np.pi * wave)) / 3.0
    return (wave**2).astype(np.float32), (1.0 / factor**2).astype(np.float32)


basis = real_basis()
columns_y = np.zeros((GRID, 4 * rows_y))
for c in range(4):
    for y in range(ext_y):
        columns_y[:, c * rows_y + y] = basis[:, (64 * c - 1 + y) % GRID]
columns_x = np.concatenate([basis[:, (4 * np.arange(64) - 1 + x) % GRID] for x in range(ext_x)], axis=1)
forward_z = split_table(basis.T.copy())
inverse_z = split_table(basis)
forward_y = split_table(columns_y)
lines_y = np.zeros((4 * rows_back, GRID))
for c in range(4):
    lines_y[c * rows_back : c * rows_back + ext_y] = columns_y[:, c * rows_y : c * rows_y + ext_y].T
inverse_y = split_table(lines_y)
forward_x = split_table(columns_x)
inverse_x = split_table(columns_x.T.copy())
wave_square, wave_factor = wave_tables()
waves = np.stack([wave_square, wave_factor])
wave_x = np.repeat(waves.reshape(2 * GRID, 1), 128, axis=1)
wave_yz = np.concatenate(
    [np.repeat(waves.reshape(2, 4, 64).transpose(0, 2, 1), 64, axis=2), np.tile(waves.reshape(2, 4, 64), (1, 1, 4)), np.zeros((2, 4, GRID), np.float32)], axis=1
).reshape(144, GRID)
narrow = np.concatenate([*forward_z, *inverse_z, *inverse_x, *inverse_y], axis=0)
wide = np.concatenate([np.pad(t, ((0, 0), (0, 512 - t.shape[1]))) for t in (*forward_y, *forward_x)], axis=0)

def halves(x):
    high = x.astype(jnp.bfloat16)
    return high, (x - high.astype(jnp.float32)).astype(jnp.bfloat16)


def dot_split(a, b, pattern=(((1,), (0,)), ((), ()))):
    dot = functools.partial(lax.dot_general, dimension_numbers=pattern, preferred_element_type=jnp.float32)
    return dot(a[0], b[0]) + (dot(a[0], b[1]) + dot(a[1], b[0]))


def spline_four(f):
    g = 1.0 - f
    f2 = f * f
    f3 = f2 * f
    return (
        g * g * g * (1.0 / 6.0),
        (3.0 * f3 - 6.0 * f2 + 4.0) * (1.0 / 6.0),
        (-3.0 * f3 + 3.0 * f2 + 3.0 * f + 1.0) * (1.0 / 6.0),
        f3 * (1.0 / 6.0),
    )


def placed_weights(count, cell, f, wraps=False):
    ids = lax.broadcasted_iota(jnp.int32, (count, cell.shape[1]), 0)
    step = ids - cell
    if wraps:
        step = (step + 1) & (GRID - 1)
    result = jnp.zeros(step.shape, jnp.float32)
    for k, weight in enumerate(spline_four(f)):
        result = jnp.where(step == k, weight, result)
    return result


def pair_tiles(first, second, half):
    lane = lax.broadcasted_iota(jnp.int32, first.shape, 1)
    if half == 0:
        return jnp.where(lane < 64, first, pltpu.roll(second, 64, 1))
    return jnp.where(lane < 64, pltpu.roll(first, 64, 1), second)


def charge_row(feat_ref, w_ref):
    f32, bf16 = jnp.float32, jnp.bfloat16
    w = jnp.broadcast_to(w_ref[...], (16, 128))
    top = w.astype(bf16).astype(f32)
    mid = (w - top).astype(bf16).astype(f32)
    sub = lax.broadcasted_iota(jnp.int32, (16, 128), 0)
    parts = jnp.where(sub == 0, top, jnp.where(sub == 1, mid, jnp.where(sub == 2, w - top - mid, 0.0))).astype(bf16)
    raw = lax.dot_general(parts, feat_ref[...], (((1,), (1,)), ((), ())), preferred_element_type=f32)
    raw = jnp.broadcast_to(raw[0:1] + raw[1:2] + raw[2:3], (8, raw.shape[1]))
    lane = lax.broadcasted_iota(jnp.int32, raw.shape, 1)
    mate = jnp.where(lane % 2 == 0, pltpu.roll(raw, raw.shape[1] - 1, 1), pltpu.roll(raw, 1, 1))
    return 0.5 * (raw - mate)


def atom_row(ref, c, i):
    return jnp.concatenate([ref[pl.ds(c * 16 + 4 * i + q, 1), :] for q in range(4)], axis=1)


def spread(cell_ref, frac_ref, charge_s, along_s, grid_s, table, out_ref):
    grid_s[...] = jnp.zeros_like(grid_s)

    def tile(i, carry):
        cols = pl.ds(pl.multiple_of(i * 512, 512), 512)
        along_x = placed_weights(8, atom_row(cell_ref, 0, i), atom_row(frac_ref, 0, i)) * charge_s[0:1, cols]
        along_y = placed_weights(rows_y, atom_row(cell_ref, 1, i), atom_row(frac_ref, 1, i))
        along_z = halves(placed_weights(GRID, atom_row(cell_ref, 2, i), atom_row(frac_ref, 2, i), True))
        along_s[0, :, cols] = along_z[0]
        along_s[1, :, cols] = along_z[1]
        plane = jnp.concatenate([along_x[x : x + 1] * along_y for x in range(ext_x)], axis=0)
        grid_s[...] += dot_split(halves(plane), along_z, (((1,), (1,)), ((), ())))
        return carry

    lax.fori_loop(0, 4, tile, 0)
    waves = dot_split(halves(grid_s[...]), table)
    for c in range(4):
        cols = slice(128 * (c // 2), 128 * (c // 2) + 128)
        slab = lambda x: waves[x * rows_y : (x + 1) * rows_y, cols]
        for q in range(3):
            out_ref[c, q * rows_y : (q + 1) * rows_y, :] = pair_tiles(slab(2 * q), slab(2 * q + 1), c % 2)
        last = slab(6)
        below = jnp.concatenate([last[40:rows_y], jnp.zeros((8, 128), jnp.float32)], axis=0)
        out_ref[c, 3 * rows_y : 3 * rows_y + 40, :] = pair_tiles(last[0:40], below, c % 2)


def forward_y_step(x_ref, table, out_ref):
    pieces = []
    for c in range(4):
        tail = x_ref[c, 3 * rows_y :, :]
        last = jnp.concatenate([tail, pltpu.roll(tail, 64, 1)[0 : rows_y - 40]], axis=0)
        pieces.append(jnp.concatenate([x_ref[c, q * rows_y : (q + 1) * rows_y, :] for q in range(3)] + [last], axis=1))
    waves = dot_split(table, halves(jnp.concatenate(pieces, axis=0)))
    for j in range(4):
        out_ref[:, 0, j * 384 : j * 384 + 384] = waves[64 * j : 64 * j + 64, 0:384]
    for p in range(2):
        tail = [waves[128 * p + 64 * q : 128 * p + 64 * q + 64, 384:512] for q in range(2)]
        out_ref[:, 0, 1536 + p * 128 : 1664 + p * 128] = pair_tiles(tail[0], tail[1], 0)


def influence_block(x_ref, yz_ref, me, part):
    spot = lambda row: yz_ref[pl.ds(row, 1), :]
    twice = lambda block: jnp.concatenate([block, block], axis=1)
    square = twice(x_ref[0:GRID, :]) + (spot(me) + spot(64 + part))
    factor = twice(x_ref[GRID:, :]) * (spot(72 + me) * spot(136 + part))
    positive = square > 0.0
    safe = jnp.where(positive, square, 1.0)
    return jnp.where(positive, 16.0 * jnp.exp(square * (-(math.pi**2))) / safe * factor, 0.0)


def filter_step(x_ref, table, back, influence_ref, turn_s, out_ref):
    pieces = []
    for x in range(ext_x - 1):
        slabs = [x_ref[:, 0, j * 384 + 128 * (x // 2) : j * 384 + 128 * (x // 2) + 128] for j in range(4)]
        pieces.append(jnp.concatenate([pair_tiles(slabs[2 * p], slabs[2 * p + 1], x % 2) for p in range(2)], axis=1))
    pieces.append(x_ref[:, 0, 1536:1792])
    waves = dot_split(table, halves(jnp.concatenate(pieces, axis=0)))
    cells = dot_split(back, halves(waves * influence_ref[...]))
    for j in range(4):
        for q in range(4):
            cols = slice(128 * (j // 2), 128 * (j // 2) + 128)
            first = cells[128 * q : 128 * q + 64, cols]
            if 2 * q + 1 < ext_x:
                second = cells[128 * q + 64 : 128 * q + 128, cols]
            else:
                second = jnp.zeros_like(first)
            turn_s[:, j * 4 + q, :] = pair_tiles(first, second, j % 2)
    out_ref[...] = turn_s[...].astype(jnp.bfloat16)


def inverse_y_step(x_ref, table, turn_s, out_ref):
    turn_s[...] = x_ref[...].astype(jnp.float32)
    data = jnp.concatenate(
        [jnp.concatenate([turn_s[:, j * 4 + q, :] for q in range(4)], axis=1) for j in range(4)], axis=0
    ).astype(jnp.bfloat16)
    dot = functools.partial(jnp.dot, preferred_element_type=jnp.float32)
    cells = dot(table[0], data) + dot(table[1], data)
    for c in range(4):
        out_ref[c] = cells[c * rows_back : (c + 1) * rows_back].astype(jnp.bfloat16)


def read_step(x_ref, cell_ref, frac_ref, along_s, table, out_ref, grid_s):
    f32 = jnp.float32
    pieces = []
    for x in range(ext_x):
        cols = slice(128 * (x // 2), 128 * (x // 2) + 128)
        slab = [x_ref[c, :, cols].astype(f32) for c in range(4)]
        pieces.append(jnp.concatenate([pair_tiles(slab[2 * p], slab[2 * p + 1], x % 2) for p in range(2)], axis=1))
    lines = jnp.concatenate(pieces, axis=0).astype(jnp.bfloat16)
    dot = functools.partial(jnp.dot, preferred_element_type=f32)
    grid_s[...] = dot(lines, table[0]) + dot(lines, table[1])

    def tile(i, carry):
        cols = pl.ds(pl.multiple_of(i * 512, 512), 512)
        along_x = placed_weights(8, atom_row(cell_ref, 0, i), atom_row(frac_ref, 0, i))
        along_y = placed_weights(rows_back, atom_row(cell_ref, 1, i), atom_row(frac_ref, 1, i))
        lines = dot_split(halves(grid_s[...]), (along_s[0, :, cols], along_s[1, :, cols]))
        total = jnp.zeros(along_y.shape, f32)
        for x in range(ext_x):
            total = total + along_x[x : x + 1] * lines[x * rows_back : (x + 1) * rows_back]
        out_ref[:, cols] = jnp.sum(total * along_y, axis=0, keepdims=True)
        return carry

    lax.fori_loop(0, 4, tile, 0)


def geometry_step(g, nb_ref, cnt_ref, geo_s, ang_s, rad_s):
    f32 = jnp.float32
    sub = lax.broadcasted_iota(jnp.int32, (8, 128), 0)
    lane = lax.broadcasted_iota(jnp.int32, (8, 128), 1)
    rows = pl.ds(pl.multiple_of(g * 8, 8), 8)
    nb = nb_ref[rows, :]
    low = nb & 127
    high = nb >> 7
    part = [jnp.zeros((8, 128), f32) for _ in range(3)]
    for h in range(48):
        hit = high == h
        for c in range(3):
            row = jnp.broadcast_to(geo_s[c * 48 + h : c * 48 + h + 1, :], (8, 128))
            part[c] = jnp.where(hit, jnp.take_along_axis(row, low, axis=1), part[c])
    centre = (g % 2) * 64 + sub * 8 + lane // 16
    spot = lambda ref, row: jnp.take_along_axis(jnp.broadcast_to(ref[pl.ds(row, 1), :], (8, 128)), centre, axis=1)
    mine = [spot(geo_s, c * 48 + g // 2) for c in range(3)]
    live = spot(cnt_ref, g // 2)
    dx = part[0] - mine[0]
    dy = part[1] - mine[1]
    dz = part[2] - mine[2]
    cells = jnp.floor(part[2]) - jnp.floor(mine[2])
    dz = jnp.where(cells >= 128.0, dz - 256.0, jnp.where(cells < -128.0, dz + 256.0, dz))
    squared = dx * dx + dy * dy + dz * dz + 1.0
    distance = jnp.sqrt(squared)
    inverse = 1.0 / distance
    nx, ny, nz = dx * inverse, dy * inverse, dz * inverse
    env = jnp.where((lane % 16) < live, 1.0 / (1.0 + squared * (1.0 / 4096.0)), 0.0)
    r3, r5, r15 = math.sqrt(3.0), math.sqrt(5.0), math.sqrt(15.0)
    ex, ey, ez = env * nx, env * ny, env * nz
    angular = [
        env, r3 * ex, r3 * ey, r3 * ez, r15 * ex * ny, r15 * ey * nz,
        (0.5 * r5) * (3.0 * ez * nz - env), r15 * ex * nz, (0.5 * r15) * (ex * nx - ey * ny),
    ]
    for m in range(9):
        ang_s[m, rows, :] = angular[m]
    for j in range(8):
        rad_s[rows, j, :] = jnp.exp(distance * (-1.0 / 2.0**j))


def gather_rows(g, r, idx_ref, tab_s, buf):
    sub = lax.broadcasted_iota(jnp.int32, (8, 128), 0)
    for t in range(r*16, r*16+16):
        acc = None
        for j in range(8):
            v = tab_s[pl.ds(idx_ref[g * 1024 + (t * 8 + j)] + (table_pad - j), 8), :]
            acc = v if acc is None else jnp.where(sub == j, v, acc)
        buf[t*8:t*8+8,:] = acc


def moments_pair(g, p, hid, ang_s, inv_all):
    f32, bf16 = jnp.float32, jnp.bfloat16
    sub = lax.broadcasted_iota(jnp.int32, (8, 128), 0)
    diag = (lax.broadcasted_iota(jnp.int32, (8, 128), 1) // 16) == sub
    zero = jnp.zeros((8, 128), f32)
    blocks_hi, blocks_lo = [], []
    for m in range(9):
        cols_hi, cols_lo = [], []
        for q in range(2):
            line = ang_s[m, pl.ds(g * 8 + (2 * p + q), 1), :]
            row = jnp.where(diag, jnp.broadcast_to(line, (8, 128)), 0.0)
            row_hi = row.astype(bf16).astype(f32)
            row_lo = row - row_hi
            cols_hi.append(jnp.concatenate([row_hi, zero] if q == 0 else [zero, row_hi], axis=0).astype(bf16))
            cols_lo.append(jnp.concatenate([row_lo, zero] if q == 0 else [zero, row_lo], axis=0).astype(bf16))
        blocks_hi.append(jnp.concatenate(cols_hi, axis=1))
        blocks_lo.append(jnp.concatenate(cols_lo, axis=1))
    both = jnp.concatenate(blocks_hi + blocks_lo, axis=0)
    mom2 = jnp.dot(both, hid, preferred_element_type=f32)
    mom = mom2[:144, :128] + mom2[:144, 128:] + mom2[144:, :128]
    sq = [mom[m * 16 : m * 16 + 16] ** 2 for m in range(9)]
    inv = jnp.concatenate([sq[0], sq[1] + sq[2] + sq[3], (sq[4] + sq[5]) + (sq[6] + sq[7]) + sq[8]], axis=1)
    inv_all[pl.ds(pl.multiple_of(g*64 + p*16,16),16), :] = inv.astype(bf16)


def edge_pipe(g, nxt, w_ext, w_mid, idx_ref, tab_s, src_s, ang_s, rad_s, buf, other, inv_all):
    f32, bf16 = jnp.float32, jnp.bfloat16
    pieces = []
    for r in range(8):
        rad = rad_s[g * 8 + r]
        rad_hi = rad.astype(bf16).astype(f32)
        pieces.append(jnp.concatenate([rad_hi, rad - rad_hi, rad_hi, jnp.zeros_like(rad)], axis=0).astype(bf16))
    rad_ext = jnp.concatenate(pieces, axis=1)
    term = lax.dot_general(rad_ext, w_ext, (((0,), (0,)), ((), ())), preferred_element_type=f32)
    lats = []
    for r in range(8):
        if nxt is not None:
            gather_rows(nxt, r, idx_ref, tab_s, other)
        src = src_s[pl.ds(pl.multiple_of(g * 64 + r*8, 8), 8), :]
        src = jnp.broadcast_to(src[:, None, :], (8, 16, 128)).reshape(128, 128)
        half = buf[r*128:r*128+128,:] + src + term[r*128:r*128+128]
        lats.append((half + half * jnp.tanh(half)).astype(bf16))
    half = jnp.dot(jnp.concatenate(lats, axis=0), w_mid, preferred_element_type=f32)
    hidden = half + half * jnp.tanh(half)
    hid = jnp.concatenate(halves(hidden), axis=1)
    for p in range(4):
        moments_pair(g, p, hid[p*256:p*256+256], ang_s, inv_all)


def finish(out_ref, own_ref, inv_all, w_out):
    def step(i, carry):
        rows = pl.ds(pl.multiple_of(i*512,512),512)
        out_ref[rows,:] = (own_ref[rows,:].astype(jnp.float32) + jnp.dot(inv_all[rows,:], w_out, preferred_element_type=jnp.float32)).astype(jnp.bfloat16)
        return carry
    lax.fori_loop(0, 4, step, 0)


def layer_kernel(
    idx_ref, own_hbm, nb_hbm, cnt_hbm, offset_hbm, frac_hbm, wcharge_hbm, wsrc_hbm, wdst_hbm, wrad_hbm, wmid_hbm,
    wout_hbm, narrow_hbm, wide_hbm, wave_x_hbm, wave_yz_hbm,
    new_ref, pot_ref,
    feat_halo, geo_halo, zsend, zrecv, ysend, yrecv, xsend, xrecv, isend, irecv,
    tab_s, src_s, geo_s, ang_s, rad_s, inv_s, grid_s, charge_s, along_s, influence_s,
    cell_s, head_s, even_s, odd_s, turn_s, back_s,
    own_ref, nb_ref, cnt_ref, offset_ref, frac_ref, wcharge_ref, wsrc_ref, wdst_ref, wrad_ref, wmid_ref,
    wout_ref, narrow_ref, wide_ref, wave_x_ref, wave_yz_ref, load_sem,
    feat_send, feat_recv, geo_send, geo_recv, zs_sem, zr_sem, ys_sem, yr_sem, xs_sem, xr_sem, is_sem, ir_sem,
):
    f32, bf16 = jnp.float32, jnp.bfloat16
    me, part = lax.axis_index("dom"), lax.axis_index("sub")
    doms, subs = 64, 4
    turn = lambda x, step, size: lax.rem(x + (step + size), size)

    sources = (
        offset_hbm, frac_hbm, own_hbm, wcharge_hbm, narrow_hbm, wsrc_hbm, wdst_hbm, wave_x_hbm, wave_yz_hbm,
        nb_hbm, cnt_hbm, wide_hbm, wrad_hbm, wmid_hbm, wout_hbm,
    )
    places = (
        offset_ref, frac_ref, own_ref, wcharge_ref, narrow_ref, wsrc_ref, wdst_ref, wave_x_ref, wave_yz_ref,
        nb_ref, cnt_ref, wide_ref, wrad_ref, wmid_ref, wout_ref,
    )
    loads = [pltpu.make_async_copy(a, b, load_sem.at[k]) for k, (a, b) in enumerate(zip(sources, places))]
    for load in loads:
        load.start()
    table = lambda at, count: (narrow_ref[at : at + count, :], narrow_ref[at + count : at + 2 * count, :])
    broad = lambda at, width: (wide_ref[at : at + GRID, 0:width], wide_ref[at + GRID : at + 2 * GRID, 0:width])

    barrier = pltpu.get_barrier_semaphore()

    def greet(dom, sub):
        pl.semaphore_signal(barrier, inc=1, device_id=(dom, sub), device_id_type=pl.DeviceIdType.MESH)

    for step_x in (-1, 1):
        for step_y in (-1, 1):
            greet(turn(me, step_x, doms), turn(part, step_y, subs))
    for step in range(1, subs):
        greet(me, turn(part, step, subs))

    def greet_dom(step, carry):
        greet(lax.rem(me + step, doms), part)
        return carry

    lax.fori_loop(1, doms, greet_dom, 0)
    for load in loads[:4]:
        load.wait()
    for c, anchor in enumerate((me * 4, part * 64, 0)):
        cell_s[c * 16 : c * 16 + 16, :] = offset_ref[c * 16 : c * 16 + 16, :] - anchor
        place = cell_s[c * 16 : c * 16 + 16, :].astype(f32) + frac_ref[c * 16 : c * 16 + 16, :]
        geo_s[c * 48 : c * 48 + 16, :] = place
        head_s[c * 4 : c * 4 + 4, :] = place[0:4]
    head_s[12:16, :] = jnp.zeros((4, 128), f32)

    charge_s[...] = charge_row(own_ref, wcharge_ref)
    pl.semaphore_wait(barrier, 4 + subs - 1 + doms - 1)

    def remote(src, dst, send, recv, dom, sub):
        return pltpu.make_async_remote_copy(
            src_ref=src, dst_ref=dst, send_sem=send, recv_sem=recv,
            device_id=(dom, sub), device_id_type=pl.DeviceIdType.MESH,
        )

    geo_copies = []
    for r, (place_x, place_y) in enumerate(halo_places):
        target = (turn(me, 1 - place_x, doms), turn(part, 1 - place_y, subs))
        geo_copies.append(remote(head_s, geo_halo.at[r], geo_send.at[r], geo_recv.at[r], *target))

    odd, high = lax.rem(part, 2), part // 2
    mate, cross = part + 1 - 2 * odd, turn(part, 2 * odd - 1, subs)
    mate_y, cross_y = 2 * odd, 2 - 2 * odd
    rows = own_ref.at[pl.ds(0, head_rows)]

    def feat_copy(k, src, slot, dom, sub):
        return remote(src, feat_halo.at[slot], feat_send.at[k], feat_recv.at[slot], dom, sub)

    def feat_wait(slot):
        remote(rows, feat_halo.at[slot], feat_send.at[0], feat_recv.at[slot], turn(me, 1, doms), part).wait_recv()

    first = [
        feat_copy(0, rows, 1, turn(me, 1, doms), part),
        feat_copy(1, rows, 7, turn(me, -1, doms), part),
        feat_copy(2, rows, 3 + cross_y, me, cross),
        feat_copy(3, rows, 6 * (1 - high) + cross_y, turn(me, 2 * high - 1, doms), cross),
        feat_copy(4, rows, 3 + mate_y, me, mate),
    ]
    second = [
        feat_copy(5, feat_halo.at[6 * high + 1], 6 * high + cross_y, me, cross),
        feat_copy(6, feat_halo.at[1], mate_y, me, mate),
        feat_copy(7, feat_halo.at[7], 6 + mate_y, me, mate),
    ]
    for copy in geo_copies + first:
        copy.start()

    def swap_sub(src, dst, send, recv):
        return [
            remote(src.at[turn(part, step, subs)], dst.at[part], send.at[step - 1], recv.at[step - 1],
                   me, turn(part, step, subs))
            for step in range(1, subs)
        ]

    def dom_copy(src, dst, send, recv, step):
        target = lax.rem(me + step, doms)
        return remote(src.at[target], dst.at[me], send.at[step - 1], recv.at[step - 1], target, part)

    def swap_dom(src, dst, send, recv):
        def start(step, carry):
            dom_copy(src, dst, send, recv, step).start()
            return carry

        lax.fori_loop(1, doms, start, 0)
        dst[me] = src[me]

    def dom_wait(src, dst, send, recv, which):
        def wait(step, carry):
            getattr(dom_copy(src, dst, send, recv, step), which)()
            return carry

        lax.fori_loop(1, doms, wait, 0)

    loads[4].wait()
    spread(cell_s, frac_ref, charge_s, along_s, grid_s, table(0, GRID), zsend)
    z_copies = swap_sub(zsend, zrecv, zs_sem, zr_sem)
    for copy in z_copies:
        copy.start()
    zrecv[part] = zsend[part]

    for load in loads[5:]:
        load.wait()
    halved = lambda ref: (ref[...].astype(f32) * 0.5).astype(bf16)
    w_src, w_dst, w_mid, w_out = halved(wsrc_ref), halved(wdst_ref), halved(wmid_ref), wout_ref[...]
    wr = wrad_ref[...] * 0.5
    wr_hi = wr.astype(bf16).astype(f32)
    w_ext = jnp.concatenate([wr_hi, wr_hi, wr - wr_hi, jnp.zeros_like(wr)], axis=0).astype(bf16)
    src_s[...] = jnp.dot(own_ref[...], w_src, preferred_element_type=f32)
    tab_s[table_pad : table_pad + 2048, :] = jnp.dot(own_ref[...], w_dst, preferred_element_type=f32)
    tab_s[0:table_pad, :] = jnp.zeros((table_pad, 128), f32)
    tab_s[table_pad + 6144 :, :] = jnp.zeros((table_pad, 128), f32)
    feat_wait(1)
    feat_wait(7)
    for copy in second:
        copy.start()
    influence_s[...] = influence_block(wave_x_ref, wave_yz_ref, me, part)
    for copy in geo_copies:
        copy.wait_recv()
    for c in range(3):
        for r, (place_x, place_y) in enumerate(halo_places):
            shift = (4.0 * (place_x - 1), 64.0 * (place_y - 1), 0.0)[c]
            at = c * 48 + 16 + r * 4
            geo_s[at : at + 4, :] = geo_halo[r, c * 4 : c * 4 + 4, :] + shift

    def geometry(g, carry):
        geometry_step(2 * g, nb_ref, cnt_ref, geo_s, ang_s, rad_s)
        geometry_step(2 * g + 1, nb_ref, cnt_ref, geo_s, ang_s, rad_s)
        return carry

    lax.fori_loop(0, 16, geometry, 0)

    for copy in z_copies:
        copy.wait_recv()
    forward_y_step(zrecv, broad(0, 4 * rows_y), ysend)
    swap_dom(ysend, yrecv, ys_sem, yr_sem)

    for slot in (0, 2, 3, 5, 6, 8):
        feat_wait(slot)
    for r, (place_x, place_y) in enumerate(halo_places):
        base = table_pad + 2048 + r * head_rows
        tab_s[base : base + head_rows, :] = jnp.dot(feat_halo[3 * place_x + place_y], w_dst, preferred_element_type=f32)

    i_copies = swap_sub(isend, irecv, is_sem, ir_sem)

    pipe = functools.partial(
        edge_pipe, w_ext=w_ext, w_mid=w_mid, idx_ref=idx_ref, tab_s=tab_s, src_s=src_s, ang_s=ang_s, rad_s=rad_s,
        inv_all=inv_s,
    )
    for r in range(8):
        gather_rows(0, r, idx_ref, tab_s, even_s)

    def edges(i, carry):
        @pl.when(i == edge_split[0])
        def _():
            dom_wait(ysend, yrecv, ys_sem, yr_sem, "wait_recv")
            filter_step(yrecv, broad(2 * GRID, 64 * ext_x), table(4 * GRID, 64 * ext_x), influence_s, turn_s, xsend)
            swap_dom(xsend, xrecv, xs_sem, xr_sem)

        @pl.when(i == edge_split[1])
        def _():
            dom_wait(xsend, xrecv, xs_sem, xr_sem, "wait_recv")
            inverse_y_step(xrecv, table(4 * GRID + 128 * ext_x, 4 * rows_back), turn_s, isend)
            for copy in i_copies:
                copy.start()
            irecv[part] = isend[part]

        pipe(2 * i, 2 * i + 1, buf=even_s, other=odd_s)
        pipe(2 * i + 1, 2 * i + 2, buf=odd_s, other=even_s)
        return carry

    lax.fori_loop(0, 15, edges, 0)
    pipe(30, 31, buf=even_s, other=odd_s)
    pipe(31, None, buf=odd_s, other=even_s)
    finish(new_ref, own_ref, inv_s, w_out)
    for copy in i_copies:
        copy.wait_recv()
    read_step(irecv, cell_s, frac_ref, along_s, table(2 * GRID, GRID), pot_ref, back_s)
    for copy in geo_copies + first + second + z_copies + i_copies:
        copy.wait_send()
    dom_wait(ysend, yrecv, ys_sem, yr_sem, "wait_send")
    dom_wait(xsend, xrecv, xs_sem, xr_sem, "wait_send")


def local(features, offsets, frac, neighbors, counts, w_src, w_dst, w_rad, w_mid, w_out, w_charge):
    f32, bf16 = jnp.float32, jnp.bfloat16
    flat = lax.optimization_barrier(neighbors.reshape(-1))
    operands = (
        flat, features[0, 0], flat.reshape(256, 128), counts.reshape(16, 128), offsets.reshape(48, 128),
        frac.reshape(48, 128), w_charge[None, :], w_src, w_dst, w_rad, w_mid, w_out, narrow, wide, wave_x, wave_yz,
    )
    vmem = pl.BlockSpec(memory_space=pltpu.VMEM)
    smem = pl.BlockSpec(memory_space=pltpu.SMEM)
    hbm = pl.BlockSpec(memory_space=pltpu.HBM)
    dma = pltpu.SemaphoreType.DMA
    slabs = pltpu.VMEM((4, 3 * rows_y + 40, 128), f32)
    pencils = pltpu.VMEM((64, 1, 1792), f32)
    backs = pltpu.VMEM((64, 16, 128), bf16)
    slabs_back = pltpu.VMEM((4, rows_back, 512), bf16)
    new_rows, potential = pl.pallas_call(
        layer_kernel,
        in_specs=[smem] + [hbm] * (len(operands) - 1),
        out_specs=(vmem, vmem),
        out_shape=(jax.ShapeDtypeStruct((2048, 128), bf16), jax.ShapeDtypeStruct((1, 2048), f32)),
        scratch_shapes=[
            pltpu.VMEM((9, head_rows, 128), bf16), pltpu.VMEM((8, 16, 128), f32),
            slabs, slabs, pencils, pencils, backs, backs, slabs_back, slabs_back,
            pltpu.VMEM((6144 + 2 * table_pad, 128), f32), pltpu.VMEM((2048, 128), f32), pltpu.VMEM((144, 128), f32),
            pltpu.VMEM((9, 256, 128), f32), pltpu.VMEM((256, 8, 128), f32), pltpu.VMEM((2048, 384), bf16),
            pltpu.VMEM((ext_x * rows_y, GRID), f32), pltpu.VMEM((8, 2048), f32), pltpu.VMEM((2, GRID, 2048), bf16),
            pltpu.VMEM((GRID, GRID), f32), pltpu.VMEM((48, 128), jnp.int32), pltpu.VMEM((16, 128), f32),
            pltpu.VMEM((1024, 128), f32), pltpu.VMEM((1024, 128), f32), pltpu.VMEM((64, 16, 128), f32),
            pltpu.VMEM((ext_x * rows_back, GRID), f32),
            *[pltpu.VMEM(x.shape, x.dtype) for x in operands[1:2] + operands[2:]], dma((15,)),
            dma((8,)), dma((9,)), dma((8,)), dma((8,)), dma((3,)), dma((3,)),
            dma((63,)), dma((63,)), dma((63,)), dma((63,)), dma((3,)), dma((3,)),
        ],
        compiler_params=pltpu.CompilerParams(
            vmem_limit_bytes=50 * 2**20, collective_id=0, has_side_effects=True
        ),
        name="layer",
    )(*operands)
    return new_rows.reshape(features.shape), potential.reshape(1, 1, 2048)


def solution(mesh):
    placed = (
        P("dom", "sub", None, None),
        P(None, "dom", "sub", None),
        P(None, "dom", "sub", None),
        P("dom", "sub", None, None),
        P("dom", "sub", None),
        P(),
        P(),
        P(),
        P(),
        P(),
        P(),
    )
    return jax.shard_map(
        local,
        mesh=mesh,
        in_specs=placed,
        out_specs=(P("dom", "sub", None, None), P("dom", "sub", None)),
        check_vma=False,
    )
```

```python
import functools
import math

import jax
import jax.numpy as jnp
import ml_dtypes
import numpy as np
from jax import lax
from jax.experimental import pallas as pl
from jax.experimental.pallas import tpu as pltpu
from jax.sharding import PartitionSpec as P

GRID = 256
ext_x = 7
ext_y = 67
rows_y = 72
rows_back = 80
head_rows = 512
table_pad = 8
edge_split = (7, 12)
halo_places = [(0, 0), (0, 1), (0, 2), (1, 0), (1, 2), (2, 0), (2, 1), (2, 2)]


def split_table(table):
    high = table.astype(ml_dtypes.bfloat16)
    low = (table - high.astype(np.float64)).astype(ml_dtypes.bfloat16)
    return high, low


def real_basis():
    cells = np.arange(GRID)
    basis = np.zeros((GRID, GRID))
    for k in range(GRID):
        wave = k if k <= GRID // 2 else k - GRID // 2
        angle = 2.0 * np.pi / GRID * ((wave * cells) % GRID)
        scale = math.sqrt((1.0 if k in (0, GRID // 2) else 2.0) / GRID)
        basis[k] = scale * (np.cos(angle) if k <= GRID // 2 else np.sin(angle))
    return basis


def wave_tables():
    index = np.arange(GRID)
    wave = np.where(index <= GRID // 2, index, index - GRID // 2) / GRID
    factor = (2.0 + np.cos(2.0 * np.pi * wave)) / 3.0
    return (wave**2).astype(np.float32), (1.0 / factor**2).astype(np.float32)


basis = real_basis()
columns_y = np.zeros((GRID, 4 * rows_y))
for c in range(4):
    for y in range(ext_y):
        columns_y[:, c * rows_y + y] = basis[:, (64 * c - 1 + y) % GRID]
columns_x = np.concatenate([basis[:, (4 * np.arange(64) - 1 + x) % GRID] for x in range(ext_x)], axis=1)
forward_z = split_table(basis.T.copy())
inverse_z = split_table(basis)
forward_y = split_table(columns_y)
lines_y = np.zeros((4 * rows_back, GRID))
for c in range(4):
    lines_y[c * rows_back : c * rows_back + ext_y] = columns_y[:, c * rows_y : c * rows_y + ext_y].T
inverse_y = split_table(lines_y)
forward_x = split_table(columns_x)
inverse_x = split_table(columns_x.T.copy())
wave_square, wave_factor = wave_tables()
waves = np.stack([wave_square, wave_factor])
wave_x = np.repeat(waves.reshape(2 * GRID, 1), 128, axis=1)
wave_yz = np.concatenate(
    [np.repeat(waves.reshape(2, 4, 64).transpose(0, 2, 1), 64, axis=2), np.tile(waves.reshape(2, 4, 64), (1, 1, 4)), np.zeros((2, 4, GRID), np.float32)], axis=1
).reshape(144, GRID)
narrow = np.concatenate([*forward_z, *inverse_z, *inverse_x, *inverse_y], axis=0)
wide = np.concatenate([np.pad(t, ((0, 0), (0, 512 - t.shape[1]))) for t in (*forward_y, *forward_x)], axis=0)

def halves(x):
    high = x.astype(jnp.bfloat16)
    return high, (x - high.astype(jnp.float32)).astype(jnp.bfloat16)


def dot_split(a, b, pattern=(((1,), (0,)), ((), ()))):
    dot = functools.partial(lax.dot_general, dimension_numbers=pattern, preferred_element_type=jnp.float32)
    return dot(a[0], b[0]) + (dot(a[0], b[1]) + dot(a[1], b[0]))


def spline_four(f):
    g = 1.0 - f
    f2 = f * f
    f3 = f2 * f
    return (
        g * g * g * (1.0 / 6.0),
        (3.0 * f3 - 6.0 * f2 + 4.0) * (1.0 / 6.0),
        (-3.0 * f3 + 3.0 * f2 + 3.0 * f + 1.0) * (1.0 / 6.0),
        f3 * (1.0 / 6.0),
    )


def placed_weights(count, cell, f, wraps=False):
    ids = lax.broadcasted_iota(jnp.int32, (count, cell.shape[1]), 0)
    step = ids - cell
    if wraps:
        step = (step + 1) & (GRID - 1)
    result = jnp.zeros(step.shape, jnp.float32)
    for k, weight in enumerate(spline_four(f)):
        result = jnp.where(step == k, weight, result)
    return result


def pair_tiles(first, second, half):
    lane = lax.broadcasted_iota(jnp.int32, first.shape, 1)
    if half == 0:
        return jnp.where(lane < 64, first, pltpu.roll(second, 64, 1))
    return jnp.where(lane < 64, pltpu.roll(first, 64, 1), second)


def charge_row(feat_ref, w_ref):
    f32, bf16 = jnp.float32, jnp.bfloat16
    w = jnp.broadcast_to(w_ref[...], (16, 128))
    top = w.astype(bf16).astype(f32)
    mid = (w - top).astype(bf16).astype(f32)
    sub = lax.broadcasted_iota(jnp.int32, (16, 128), 0)
    parts = jnp.where(sub == 0, top, jnp.where(sub == 1, mid, jnp.where(sub == 2, w - top - mid, 0.0))).astype(bf16)
    raw = lax.dot_general(parts, feat_ref[...], (((1,), (1,)), ((), ())), preferred_element_type=f32)
    raw = jnp.broadcast_to(raw[0:1] + raw[1:2] + raw[2:3], (8, raw.shape[1]))
    lane = lax.broadcasted_iota(jnp.int32, raw.shape, 1)
    mate = jnp.where(lane % 2 == 0, pltpu.roll(raw, raw.shape[1] - 1, 1), pltpu.roll(raw, 1, 1))
    return 0.5 * (raw - mate)


def atom_row(ref, c, i):
    return jnp.concatenate([ref[pl.ds(c * 16 + 4 * i + q, 1), :] for q in range(4)], axis=1)


def spread(cell_ref, frac_ref, charge_s, along_s, grid_s, table, out_ref):
    grid_s[...] = jnp.zeros_like(grid_s)

    def tile(i, carry):
        cols = pl.ds(pl.multiple_of(i * 512, 512), 512)
        along_x = placed_weights(8, atom_row(cell_ref, 0, i), atom_row(frac_ref, 0, i)) * charge_s[0:1, cols]
        along_y = placed_weights(rows_y, atom_row(cell_ref, 1, i), atom_row(frac_ref, 1, i))
        along_z = halves(placed_weights(GRID, atom_row(cell_ref, 2, i), atom_row(frac_ref, 2, i), True))
        along_s[0, :, cols] = along_z[0]
        along_s[1, :, cols] = along_z[1]
        plane = jnp.concatenate([along_x[x : x + 1] * along_y for x in range(ext_x)], axis=0)
        grid_s[...] += dot_split(halves(plane), along_z, (((1,), (1,)), ((), ())))
        return carry

    lax.fori_loop(0, 4, tile, 0)
    waves = dot_split(halves(grid_s[...]), table)
    for c in range(4):
        cols = slice(128 * (c // 2), 128 * (c // 2) + 128)
        slab = lambda x: waves[x * rows_y : (x + 1) * rows_y, cols]
        for q in range(3):
            out_ref[c, q * rows_y : (q + 1) * rows_y, :] = pair_tiles(slab(2 * q), slab(2 * q + 1), c % 2)
        last = slab(6)
        below = jnp.concatenate([last[40:rows_y], jnp.zeros((8, 128), jnp.float32)], axis=0)
        out_ref[c, 3 * rows_y : 3 * rows_y + 40, :] = pair_tiles(last[0:40], below, c % 2)


def forward_y_step(x_ref, table, out_ref):
    pieces = []
    for c in range(4):
        tail = x_ref[c, 3 * rows_y :, :]
        last = jnp.concatenate([tail, pltpu.roll(tail, 64, 1)[0 : rows_y - 40]], axis=0)
        pieces.append(jnp.concatenate([x_ref[c, q * rows_y : (q + 1) * rows_y, :] for q in range(3)] + [last], axis=1))
    waves = dot_split(table, halves(jnp.concatenate(pieces, axis=0)))
    for j in range(4):
        out_ref[:, 0, j * 384 : j * 384 + 384] = waves[64 * j : 64 * j + 64, 0:384]
    for p in range(2):
        tail = [waves[128 * p + 64 * q : 128 * p + 64 * q + 64, 384:512] for q in range(2)]
        out_ref[:, 0, 1536 + p * 128 : 1664 + p * 128] = pair_tiles(tail[0], tail[1], 0)


def influence_block(x_ref, yz_ref, me, part):
    spot = lambda row: yz_ref[pl.ds(row, 1), :]
    twice = lambda block: jnp.concatenate([block, block], axis=1)
    square = twice(x_ref[0:GRID, :]) + (spot(me) + spot(64 + part))
    factor = twice(x_ref[GRID:, :]) * (spot(72 + me) * spot(136 + part))
    positive = square > 0.0
    safe = jnp.where(positive, square, 1.0)
    return jnp.where(positive, 16.0 * jnp.exp(square * (-(math.pi**2))) / safe * factor, 0.0)


def filter_step(x_ref, table, back, influence_ref, turn_s, out_ref):
    pieces = []
    for x in range(ext_x - 1):
        slabs = [x_ref[:, 0, j * 384 + 128 * (x // 2) : j * 384 + 128 * (x // 2) + 128] for j in range(4)]
        pieces.append(jnp.concatenate([pair_tiles(slabs[2 * p], slabs[2 * p + 1], x % 2) for p in range(2)], axis=1))
    pieces.append(x_ref[:, 0, 1536:1792])
    waves = dot_split(table, halves(jnp.concatenate(pieces, axis=0)))
    cells = dot_split(back, halves(waves * influence_ref[...]))
    for j in range(4):
        for q in range(4):
            cols = slice(128 * (j // 2), 128 * (j // 2) + 128)
            first = cells[128 * q : 128 * q + 64, cols]
            if 2 * q + 1 < ext_x:
                second = cells[128 * q + 64 : 128 * q + 128, cols]
            else:
                second = jnp.zeros_like(first)
            turn_s[:, j * 4 + q, :] = pair_tiles(first, second, j % 2)
    out_ref[...] = turn_s[...].astype(jnp.bfloat16)


def inverse_y_step(x_ref, table, turn_s, out_ref):
    turn_s[...] = x_ref[...].astype(jnp.float32)
    data = jnp.concatenate(
        [jnp.concatenate([turn_s[:, j * 4 + q, :] for q in range(4)], axis=1) for j in range(4)], axis=0
    ).astype(jnp.bfloat16)
    dot = functools.partial(jnp.dot, preferred_element_type=jnp.float32)
    cells = dot(table[0], data) + dot(table[1], data)
    for c in range(4):
        out_ref[c] = cells[c * rows_back : (c + 1) * rows_back].astype(jnp.bfloat16)


def read_step(x_ref, cell_ref, frac_ref, along_s, table, out_ref, grid_s):
    f32 = jnp.float32
    pieces = []
    for x in range(ext_x):
        cols = slice(128 * (x // 2), 128 * (x // 2) + 128)
        slab = [x_ref[c, :, cols].astype(f32) for c in range(4)]
        pieces.append(jnp.concatenate([pair_tiles(slab[2 * p], slab[2 * p + 1], x % 2) for p in range(2)], axis=1))
    lines = jnp.concatenate(pieces, axis=0).astype(jnp.bfloat16)
    dot = functools.partial(jnp.dot, preferred_element_type=f32)
    grid_s[...] = dot(lines, table[0]) + dot(lines, table[1])

    def tile(i, carry):
        cols = pl.ds(pl.multiple_of(i * 512, 512), 512)
        along_x = placed_weights(8, atom_row(cell_ref, 0, i), atom_row(frac_ref, 0, i))
        along_y = placed_weights(rows_back, atom_row(cell_ref, 1, i), atom_row(frac_ref, 1, i))
        lines = dot_split(halves(grid_s[...]), (along_s[0, :, cols], along_s[1, :, cols]))
        total = jnp.zeros(along_y.shape, f32)
        for x in range(ext_x):
            total = total + along_x[x : x + 1] * lines[x * rows_back : (x + 1) * rows_back]
        out_ref[:, cols] = jnp.sum(total * along_y, axis=0, keepdims=True)
        return carry

    lax.fori_loop(0, 4, tile, 0)


def geometry_step(g, nb_ref, cnt_ref, geo_s, ang_s, rad_s):
    f32 = jnp.float32
    sub = lax.broadcasted_iota(jnp.int32, (8, 128), 0)
    lane = lax.broadcasted_iota(jnp.int32, (8, 128), 1)
    rows = pl.ds(pl.multiple_of(g * 8, 8), 8)
    nb = nb_ref[rows, :]
    low = nb & 127
    high = nb >> 7
    part = [jnp.zeros((8, 128), f32) for _ in range(3)]
    for h in range(48):
        hit = high == h
        for c in range(3):
            row = jnp.broadcast_to(geo_s[c * 48 + h : c * 48 + h + 1, :], (8, 128))
            part[c] = jnp.where(hit, jnp.take_along_axis(row, low, axis=1), part[c])
    centre = (g % 2) * 64 + sub * 8 + lane // 16
    spot = lambda ref, row: jnp.take_along_axis(jnp.broadcast_to(ref[pl.ds(row, 1), :], (8, 128)), centre, axis=1)
    mine = [spot(geo_s, c * 48 + g // 2) for c in range(3)]
    live = spot(cnt_ref, g // 2)
    dx = part[0] - mine[0]
    dy = part[1] - mine[1]
    dz = part[2] - mine[2]
    cells = jnp.floor(part[2]) - jnp.floor(mine[2])
    dz = jnp.where(cells >= 128.0, dz - 256.0, jnp.where(cells < -128.0, dz + 256.0, dz))
    squared = dx * dx + dy * dy + dz * dz + 1.0
    distance = jnp.sqrt(squared)
    inverse = 1.0 / distance
    nx, ny, nz = dx * inverse, dy * inverse, dz * inverse
    env = jnp.where((lane % 16) < live, 1.0 / (1.0 + squared * (1.0 / 4096.0)), 0.0)
    r3, r5, r15 = math.sqrt(3.0), math.sqrt(5.0), math.sqrt(15.0)
    ex, ey, ez = env * nx, env * ny, env * nz
    angular = [
        env, r3 * ex, r3 * ey, r3 * ez, r15 * ex * ny, r15 * ey * nz,
        (0.5 * r5) * (3.0 * ez * nz - env), r15 * ex * nz, (0.5 * r15) * (ex * nx - ey * ny),
    ]
    for m in range(9):
        ang_s[m, rows, :] = angular[m]
    for j in range(8):
        rad_s[rows, j, :] = jnp.exp(distance * (-1.0 / 2.0**j))


def gather_rows(g, r, idx_ref, tab_s, buf):
    sub = lax.broadcasted_iota(jnp.int32, (8, 128), 0)
    for t in range(r*16, r*16+16):
        acc = None
        for j in range(8):
            v = tab_s[pl.ds(idx_ref[g * 1024 + (t * 8 + j)] + (table_pad - j), 8), :]
            acc = v if acc is None else jnp.where(sub == j, v, acc)
        buf[t*8:t*8+8,:] = acc


def moments_pair(g, p, hid, ang_s, inv_all):
    f32, bf16 = jnp.float32, jnp.bfloat16
    sub = lax.broadcasted_iota(jnp.int32, (8, 128), 0)
    diag = (lax.broadcasted_iota(jnp.int32, (8, 128), 1) // 16) == sub
    zero = jnp.zeros((8, 128), f32)
    blocks_hi, blocks_lo = [], []
    for m in range(9):
        cols_hi, cols_lo = [], []
        for q in range(2):
            line = ang_s[m, pl.ds(g * 8 + (2 * p + q), 1), :]
            row = jnp.where(diag, jnp.broadcast_to(line, (8, 128)), 0.0)
            row_hi = row.astype(bf16).astype(f32)
            row_lo = row - row_hi
            cols_hi.append(jnp.concatenate([row_hi, zero] if q == 0 else [zero, row_hi], axis=0).astype(bf16))
            cols_lo.append(jnp.concatenate([row_lo, zero] if q == 0 else [zero, row_lo], axis=0).astype(bf16))
        blocks_hi.append(jnp.concatenate(cols_hi, axis=1))
        blocks_lo.append(jnp.concatenate(cols_lo, axis=1))
    both = jnp.concatenate(blocks_hi + blocks_lo, axis=0)
    mom2 = jnp.dot(both, hid, preferred_element_type=f32)
    mom = mom2[:144, :128] + mom2[:144, 128:] + mom2[144:, :128]
    sq = [mom[m * 16 : m * 16 + 16] ** 2 for m in range(9)]
    inv = jnp.concatenate([sq[0], sq[1] + sq[2] + sq[3], (sq[4] + sq[5]) + (sq[6] + sq[7]) + sq[8]], axis=1)
    inv_all[pl.ds(pl.multiple_of(g*64 + p*16,16),16), :] = inv.astype(bf16)


def edge_pipe(g, nxt, w_ext, w_mid, idx_ref, tab_s, src_s, ang_s, rad_s, buf, other, inv_all):
    f32, bf16 = jnp.float32, jnp.bfloat16
    pieces = []
    for r in range(8):
        rad = rad_s[g * 8 + r]
        rad_hi = rad.astype(bf16).astype(f32)
        pieces.append(jnp.concatenate([rad_hi, rad - rad_hi, rad_hi, jnp.zeros_like(rad)], axis=0).astype(bf16))
    rad_ext = jnp.concatenate(pieces, axis=1)
    term = lax.dot_general(rad_ext, w_ext, (((0,), (0,)), ((), ())), preferred_element_type=f32)
    lats = []
    for r in range(8):
        if nxt is not None:
            gather_rows(nxt, r, idx_ref, tab_s, other)
        src = src_s[pl.ds(pl.multiple_of(g * 64 + r*8, 8), 8), :]
        src = jnp.broadcast_to(src[:, None, :], (8, 16, 128)).reshape(128, 128)
        half = buf[r*128:r*128+128,:] + src + term[r*128:r*128+128]
        lats.append((half + half * jnp.tanh(half)).astype(bf16))
    half = jnp.dot(jnp.concatenate(lats, axis=0), w_mid, preferred_element_type=f32)
    hidden = half + half * jnp.tanh(half)
    hid = jnp.concatenate(halves(hidden), axis=1)
    for p in range(4):
        moments_pair(g, p, hid[p*256:p*256+256], ang_s, inv_all)


def finish(out_ref, own_ref, inv_all, w_out):
    def step(i, carry):
        rows = pl.ds(pl.multiple_of(i*512,512),512)
        out_ref[rows,:] = (own_ref[rows,:].astype(jnp.float32) + jnp.dot(inv_all[rows,:], w_out, preferred_element_type=jnp.float32)).astype(jnp.bfloat16)
        return carry
    lax.fori_loop(0, 4, step, 0)


def layer_kernel(
    idx_ref, own_hbm, nb_hbm, cnt_hbm, offset_hbm, frac_hbm, wcharge_hbm, wsrc_hbm, wdst_hbm, wrad_hbm, wmid_hbm,
    wout_hbm, narrow_hbm, wide_hbm, wave_x_hbm, wave_yz_hbm,
    new_ref, pot_ref,
    feat_halo, geo_halo, zsend, zrecv, ysend, yrecv, xsend, xrecv, isend, irecv,
    tab_s, src_s, geo_s, ang_s, rad_s, inv_s, grid_s, charge_s, along_s, influence_s,
    cell_s, head_s, even_s, odd_s, turn_s, back_s,
    own_ref, nb_ref, cnt_ref, offset_ref, frac_ref, wcharge_ref, wsrc_ref, wdst_ref, wrad_ref, wmid_ref,
    wout_ref, narrow_ref, wide_ref, wave_x_ref, wave_yz_ref, load_sem,
    feat_send, feat_recv, geo_send, geo_recv, zs_sem, zr_sem, ys_sem, yr_sem, xs_sem, xr_sem, is_sem, ir_sem,
):
    f32, bf16 = jnp.float32, jnp.bfloat16
    me, part = lax.axis_index("dom"), lax.axis_index("sub")
    doms, subs = 64, 4
    turn = lambda x, step, size: lax.rem(x + (step + size), size)

    sources = (
        offset_hbm, frac_hbm, own_hbm, wcharge_hbm, narrow_hbm, wsrc_hbm, wdst_hbm, wave_x_hbm, wave_yz_hbm,
        nb_hbm, cnt_hbm, wide_hbm, wrad_hbm, wmid_hbm, wout_hbm,
    )
    places = (
        offset_ref, frac_ref, own_ref, wcharge_ref, narrow_ref, wsrc_ref, wdst_ref, wave_x_ref, wave_yz_ref,
        nb_ref, cnt_ref, wide_ref, wrad_ref, wmid_ref, wout_ref,
    )
    loads = [pltpu.make_async_copy(a, b, load_sem.at[k]) for k, (a, b) in enumerate(zip(sources, places))]
    for load in loads:
        load.start()
    table = lambda at, count: (narrow_ref[at : at + count, :], narrow_ref[at + count : at + 2 * count, :])
    broad = lambda at, width: (wide_ref[at : at + GRID, 0:width], wide_ref[at + GRID : at + 2 * GRID, 0:width])

    barrier = pltpu.get_barrier_semaphore()

    def greet(dom, sub):
        pl.semaphore_signal(barrier, inc=1, device_id=(dom, sub), device_id_type=pl.DeviceIdType.MESH)

    for step_x in (-1, 1):
        for step_y in (-1, 1):
            greet(turn(me, step_x, doms), turn(part, step_y, subs))
    for step in range(1, subs):
        greet(me, turn(part, step, subs))

    def greet_dom(step, carry):
        greet(lax.rem(me + step, doms), part)
        return carry

    lax.fori_loop(1, doms, greet_dom, 0)
    for load in loads[:4]:
        load.wait()
    for c, anchor in enumerate((me * 4, part * 64, 0)):
        cell_s[c * 16 : c * 16 + 16, :] = offset_ref[c * 16 : c * 16 + 16, :] - anchor
        place = cell_s[c * 16 : c * 16 + 16, :].astype(f32) + frac_ref[c * 16 : c * 16 + 16, :]
        geo_s[c * 48 : c * 48 + 16, :] = place
        head_s[c * 4 : c * 4 + 4, :] = place[0:4]
    head_s[12:16, :] = jnp.zeros((4, 128), f32)

    charge_s[...] = charge_row(own_ref, wcharge_ref)
    pl.semaphore_wait(barrier, 4 + subs - 1 + doms - 1)

    def remote(src, dst, send, recv, dom, sub):
        return pltpu.make_async_remote_copy(
            src_ref=src, dst_ref=dst, send_sem=send, recv_sem=recv,
            device_id=(dom, sub), device_id_type=pl.DeviceIdType.MESH,
        )

    geo_copies = []
    for r, (place_x, place_y) in enumerate(halo_places):
        target = (turn(me, 1 - place_x, doms), turn(part, 1 - place_y, subs))
        geo_copies.append(remote(head_s, geo_halo.at[r], geo_send.at[r], geo_recv.at[r], *target))

    odd, high = lax.rem(part, 2), part // 2
    mate, cross = part + 1 - 2 * odd, turn(part, 2 * odd - 1, subs)
    mate_y, cross_y = 2 * odd, 2 - 2 * odd
    rows = own_ref.at[pl.ds(0, head_rows)]

    def feat_copy(k, src, slot, dom, sub):
        return remote(src, feat_halo.at[slot], feat_send.at[k], feat_recv.at[slot], dom, sub)

    def feat_wait(slot):
        remote(rows, feat_halo.at[slot], feat_send.at[0], feat_recv.at[slot], turn(me, 1, doms), part).wait_recv()

    first = [
        feat_copy(0, rows, 1, turn(me, 1, doms), part),
        feat_copy(1, rows, 7, turn(me, -1, doms), part),
        feat_copy(2, rows, 3 + cross_y, me, cross),
        feat_copy(3, rows, 6 * (1 - high) + cross_y, turn(me, 2 * high - 1, doms), cross),
        feat_copy(4, rows, 3 + mate_y, me, mate),
    ]
    second = [
        feat_copy(5, feat_halo.at[6 * high + 1], 6 * high + cross_y, me, cross),
        feat_copy(6, feat_halo.at[1], mate_y, me, mate),
        feat_copy(7, feat_halo.at[7], 6 + mate_y, me, mate),
    ]
    for copy in geo_copies + first:
        copy.start()

    def swap_sub(src, dst, send, recv):
        return [
            remote(src.at[turn(part, step, subs)], dst.at[part], send.at[step - 1], recv.at[step - 1],
                   me, turn(part, step, subs))
            for step in range(1, subs)
        ]

    def dom_copy(src, dst, send, recv, step):
        target = lax.rem(me + step, doms)
        return remote(src.at[target], dst.at[me], send.at[0], recv.at[0], target, part)

    def swap_dom(src, dst, send, recv):
        def start(step, carry):
            dom_copy(src, dst, send, recv, step).start()
            return carry

        lax.fori_loop(1, doms, start, 0)
        dst[me] = src[me]

    def dom_wait(src, dst, send, recv, which):
        every = pl.ds(0, doms - 1)
        copy = remote(src.at[every], dst.at[every], send.at[0], recv.at[0], turn(me, 1, doms), part)
        getattr(copy, which)()

    loads[4].wait()
    spread(cell_s, frac_ref, charge_s, along_s, grid_s, table(0, GRID), zsend)
    z_copies = swap_sub(zsend, zrecv, zs_sem, zr_sem)
    for copy in z_copies:
        copy.start()
    zrecv[part] = zsend[part]

    for load in loads[5:]:
        load.wait()
    halved = lambda ref: (ref[...].astype(f32) * 0.5).astype(bf16)
    w_src, w_dst, w_mid, w_out = halved(wsrc_ref), halved(wdst_ref), halved(wmid_ref), wout_ref[...]
    wr = wrad_ref[...] * 0.5
    wr_hi = wr.astype(bf16).astype(f32)
    w_ext = jnp.concatenate([wr_hi, wr_hi, wr - wr_hi, jnp.zeros_like(wr)], axis=0).astype(bf16)
    src_s[...] = jnp.dot(own_ref[...], w_src, preferred_element_type=f32)
    tab_s[table_pad : table_pad + 2048, :] = jnp.dot(own_ref[...], w_dst, preferred_element_type=f32)
    tab_s[0:table_pad, :] = jnp.zeros((table_pad, 128), f32)
    tab_s[table_pad + 6144 :, :] = jnp.zeros((table_pad, 128), f32)
    feat_wait(1)
    feat_wait(7)
    for copy in second:
        copy.start()
    influence_s[...] = influence_block(wave_x_ref, wave_yz_ref, me, part)
    for copy in geo_copies:
        copy.wait_recv()
    for c in range(3):
        for r, (place_x, place_y) in enumerate(halo_places):
            shift = (4.0 * (place_x - 1), 64.0 * (place_y - 1), 0.0)[c]
            at = c * 48 + 16 + r * 4
            geo_s[at : at + 4, :] = geo_halo[r, c * 4 : c * 4 + 4, :] + shift

    def geometry(g, carry):
        geometry_step(2 * g, nb_ref, cnt_ref, geo_s, ang_s, rad_s)
        geometry_step(2 * g + 1, nb_ref, cnt_ref, geo_s, ang_s, rad_s)
        return carry

    lax.fori_loop(0, 16, geometry, 0)

    for copy in z_copies:
        copy.wait_recv()
    forward_y_step(zrecv, broad(0, 4 * rows_y), ysend)
    swap_dom(ysend, yrecv, ys_sem, yr_sem)
    for slot in (0, 2, 3, 5, 6, 8):
        feat_wait(slot)
    for r, (place_x, place_y) in enumerate(halo_places):
        base = table_pad + 2048 + r * head_rows
        tab_s[base : base + head_rows, :] = jnp.dot(feat_halo[3 * place_x + place_y], w_dst, preferred_element_type=f32)

    i_copies = swap_sub(isend, irecv, is_sem, ir_sem)

    pipe = functools.partial(
        edge_pipe, w_ext=w_ext, w_mid=w_mid, idx_ref=idx_ref, tab_s=tab_s, src_s=src_s, ang_s=ang_s, rad_s=rad_s,
        inv_all=inv_s,
    )
    for r in range(8):
        gather_rows(0, r, idx_ref, tab_s, even_s)

    def edges(i, carry):
        @pl.when(i == edge_split[0])
        def _():
            dom_wait(ysend, yrecv, ys_sem, yr_sem, "wait_recv")
            filter_step(yrecv, broad(2 * GRID, 64 * ext_x), table(4 * GRID, 64 * ext_x), influence_s, turn_s, xsend)
            swap_dom(xsend, xrecv, xs_sem, xr_sem)

        @pl.when(i == edge_split[1])
        def _():
            dom_wait(xsend, xrecv, xs_sem, xr_sem, "wait_recv")
            inverse_y_step(xrecv, table(4 * GRID + 128 * ext_x, 4 * rows_back), turn_s, isend)
            for copy in i_copies:
                copy.start()
            irecv[part] = isend[part]

        pipe(2 * i, 2 * i + 1, buf=even_s, other=odd_s)
        pipe(2 * i + 1, 2 * i + 2, buf=odd_s, other=even_s)
        return carry

    lax.fori_loop(0, 15, edges, 0)
    pipe(30, 31, buf=even_s, other=odd_s)
    pipe(31, None, buf=odd_s, other=even_s)
    finish(new_ref, own_ref, inv_s, w_out)
    for copy in i_copies:
        copy.wait_recv()
    read_step(irecv, cell_s, frac_ref, along_s, table(2 * GRID, GRID), pot_ref, back_s)
    for copy in geo_copies + first + second + z_copies + i_copies:
        copy.wait_send()
    dom_wait(ysend, yrecv, ys_sem, yr_sem, "wait_send")
    dom_wait(xsend, xrecv, xs_sem, xr_sem, "wait_send")


def local(features, offsets, frac, neighbors, counts, w_src, w_dst, w_rad, w_mid, w_out, w_charge):
    f32, bf16 = jnp.float32, jnp.bfloat16
    flat = lax.optimization_barrier(neighbors.reshape(-1))
    operands = (
        flat, features[0, 0], flat.reshape(256, 128), counts.reshape(16, 128), offsets.reshape(48, 128),
        frac.reshape(48, 128), w_charge[None, :], w_src, w_dst, w_rad, w_mid, w_out, narrow, wide, wave_x, wave_yz,
    )
    vmem = pl.BlockSpec(memory_space=pltpu.VMEM)
    smem = pl.BlockSpec(memory_space=pltpu.SMEM)
    hbm = pl.BlockSpec(memory_space=pltpu.HBM)
    dma = pltpu.SemaphoreType.DMA
    slabs = pltpu.VMEM((4, 3 * rows_y + 40, 128), f32)
    pencils = pltpu.VMEM((64, 1, 1792), f32)
    backs = pltpu.VMEM((64, 16, 128), bf16)
    slabs_back = pltpu.VMEM((4, rows_back, 512), bf16)
    new_rows, potential = pl.pallas_call(
        layer_kernel,
        in_specs=[smem] + [hbm] * (len(operands) - 1),
        out_specs=(vmem, vmem),
        out_shape=(jax.ShapeDtypeStruct((2048, 128), bf16), jax.ShapeDtypeStruct((1, 2048), f32)),
        scratch_shapes=[
            pltpu.VMEM((9, head_rows, 128), bf16), pltpu.VMEM((8, 16, 128), f32),
            slabs, slabs, pencils, pencils, backs, backs, slabs_back, slabs_back,
            pltpu.VMEM((6144 + 2 * table_pad, 128), f32), pltpu.VMEM((2048, 128), f32), pltpu.VMEM((144, 128), f32),
            pltpu.VMEM((9, 256, 128), f32), pltpu.VMEM((256, 8, 128), f32), pltpu.VMEM((2048, 384), bf16),
            pltpu.VMEM((ext_x * rows_y, GRID), f32), pltpu.VMEM((8, 2048), f32), pltpu.VMEM((2, GRID, 2048), bf16),
            pltpu.VMEM((GRID, GRID), f32), pltpu.VMEM((48, 128), jnp.int32), pltpu.VMEM((16, 128), f32),
            pltpu.VMEM((1024, 128), f32), pltpu.VMEM((1024, 128), f32), pltpu.VMEM((64, 16, 128), f32),
            pltpu.VMEM((ext_x * rows_back, GRID), f32),
            *[pltpu.VMEM(x.shape, x.dtype) for x in operands[1:2] + operands[2:]], dma((15,)),
            dma((8,)), dma((9,)), dma((8,)), dma((8,)), dma((3,)), dma((3,)),
            dma((1,)), dma((1,)), dma((1,)), dma((1,)), dma((3,)), dma((3,)),
        ],
        compiler_params=pltpu.CompilerParams(
            vmem_limit_bytes=50 * 2**20, collective_id=0, has_side_effects=True
        ),
        name="layer",
    )(*operands)
    return new_rows.reshape(features.shape), potential.reshape(1, 1, 2048)


def solution(mesh):
    placed = (
        P("dom", "sub", None, None),
        P(None, "dom", "sub", None),
        P(None, "dom", "sub", None),
        P("dom", "sub", None, None),
        P("dom", "sub", None),
        P(),
        P(),
        P(),
        P(),
        P(),
        P(),
    )
    return jax.shard_map(
        local,
        mesh=mesh,
        in_specs=placed,
        out_specs=(P("dom", "sub", None, None), P("dom", "sub", None)),
        check_vma=False,
    )
```
